256 devices in a mesh: dp: 64 (over z, x_lo, y), mp: 4 (over x_hi, core).
Axes of the slice: x: 4 (x_hi: 2, x_lo: 2; x = x_hi * 2 + x_lo), y: 4, z: 8, core: 2. Of those that a mesh axis runs over, the one named last changes fastest.
Arguments:
- image_features: bfloat16 [10240, 1152], P('dp'), may hold values from -36 to 36
- text_features: bfloat16 [10240, 1152], P('dp'), may hold values from -36 to 36
- image_proj: bfloat16 [1152, 1152], P(None, 'mp'), may hold values from -0.75 to 0.75
- text_proj: bfloat16 [1152, 1152], P(None, 'mp'), may hold values from -0.75 to 0.75
- log_scale: float32 [1], replicated, may hold values from 4.3 to 4.7
- bias: float32 [1], replicated, may hold values from -11 to -9
Outputs:
- grad_image_features: float32 [10240, 1152], P('dp', 'mp')
- grad_text_features: float32 [10240, 1152], P('dp', 'mp')
- grad_image_proj: float32 [1152, 1152], P('dp', 'mp')
- grad_text_proj: float32 [1152, 1152], P('dp', 'mp')
The draws below stay inside these ranges and needn't reach their ends.
All inputs are finite; a program needn't handle non-finite values.
Results may differ from the reference program's by a relative error of at most 0.0075.
Values may be sent and summed in bfloat16 or wider, within the bound.
No kernel may reach another device: no remote copies, remote signals or barrier semaphores. Data moves between devices by JAX's collectives and lax.ppermute only.
A program may use at most 128 MiB of HBM per device.

```python
import math
import jax
import jax.numpy as jnp
from jax import lax

D = 1152
E = 1152
TOK_DEV = 160
TOKENS = 10240


def scaled_entries(key, entries, spread):
    row_key, col_key = jax.random.split(key)
    row_scale = jnp.exp(jax.random.uniform(row_key, (TOKENS, 1), jnp.float32, -spread, spread))
    col_scale = jnp.exp(jax.random.uniform(col_key, (1, D), jnp.float32, -math.log(3.0), math.log(3.0)))
    return entries * row_scale * col_scale


def draw_image_features(key, part):
    key = jax.random.fold_in(key, 11)
    entry_key, scale_key = jax.random.split(key)
    entries = jnp.clip(jax.random.normal(entry_key, (TOKENS, D), jnp.float32), -4.0, 4.0)
    spread = math.log(3.0)
    return scaled_entries(scale_key, entries, spread).astype(jnp.bfloat16)


def draw_text_features(key, part):
    key = jax.random.fold_in(key, 23)
    entry_key, scale_key = jax.random.split(key)
    entries = jnp.clip(jax.random.normal(entry_key, (TOKENS, D), jnp.float32), -4.0, 4.0)
    spread = math.log(3.0)
    return scaled_entries(scale_key, entries, spread).astype(jnp.bfloat16)


def level_of(own_key, shape, pieces, smallest, top_value):
    loudness = 1.0
    for axis_at, parts in pieces:
        heights = jax.random.uniform(jax.random.fold_in(jax.random.fold_in(own_key, 6), axis_at), (parts,), jnp.float32, smallest / len(pieces), top_value / len(pieces))
        loudness = loudness * jnp.repeat(jnp.exp(heights), shape[axis_at] // parts).reshape((-1,) + (1,) * (len(shape) - 1 - axis_at))
    return loudness


def scatter_about(rng, dims, width, limit, cuts=(), kind=jnp.bfloat16):
    values = width * jax.random.normal(rng, dims, jnp.float32)
    if cuts:
        values = values * level_of(rng, dims, cuts, -0.22, 0.18)
    return jnp.clip(values, -limit, limit).astype(kind)


def setup_inputs(seed: int = 0) -> dict:
    keys = jax.random.split(jax.random.key(seed), 7)
    image_features = draw_image_features(jax.random.fold_in(keys[6], 71), 0)
    text_features = draw_text_features(jax.random.fold_in(keys[6], 71), 0)
    image_proj = scatter_about(keys[2], (D, E), (D // 16) ** -0.5, 0.75, ((1, 4),))
    text_proj = scatter_about(keys[3], (D, E), (D // 16) ** -0.5, 0.75, ((1, 4),))
    log_scale = jnp.clip(jax.random.uniform(keys[4], (1,), jnp.float32, 4.3, 4.7), 4.3, 4.7)
    bias = jnp.clip(jax.random.uniform(keys[5], (1,), jnp.float32, -11.0, -9.0), -11.0, -9.0)
    return {"image_features": image_features, "text_features": text_features, "image_proj": image_proj, "text_proj": text_proj, "log_scale": log_scale, "bias": bias}


def project(features, weights):
    projected = jnp.dot(features, weights, preferred_element_type=jnp.float32)
    inverse = lax.rsqrt(lax.optimization_barrier(jnp.sum(projected * projected, axis=1, keepdims=True)) + 1e-06)
    return ((projected * inverse).astype(jnp.bfloat16), inverse)

def normal_back(embedded, grads, inverse):
    values = embedded.astype(jnp.float32)
    inner = lax.optimization_barrier(jnp.sum(values * grads, axis=1, keepdims=True))
    return (inverse * (grads - values * inner)).astype(jnp.bfloat16)

def reference(image_features, text_features, image_proj, text_proj, log_scale, bias):
    z_img, r_img = project(image_features, image_proj)
    z_txt, r_txt = project(text_features, text_proj)
    scale = jnp.exp(log_scale[0])
    offset = bias[0]
    blocks = TOKENS // TOK_DEV
    image_blocks = z_img.reshape(blocks, TOK_DEV, E)
    columns = jnp.arange(TOKENS, dtype=jnp.int32)[None, :]

    def visit(carry, item):
        block, index = item
        logits = scale * jnp.dot(block, z_txt.T, preferred_element_type=jnp.float32) + offset
        rows_here = index * TOK_DEV + jnp.arange(TOK_DEV, dtype=jnp.int32)[:, None]
        sign = jnp.where(rows_here == columns, jnp.float32(1.0), jnp.float32(-1.0))
        coef = (-sign * jax.nn.sigmoid(-sign * logits) * scale).astype(jnp.bfloat16)
        grad_block = jnp.dot(coef, z_txt, preferred_element_type=jnp.float32)
        carry = carry + jnp.dot(coef.T, block, preferred_element_type=jnp.float32)
        return (carry, grad_block)
    gz_txt, gz_img = lax.scan(visit, jnp.zeros((TOKENS, E), jnp.float32), (image_blocks, jnp.arange(blocks, dtype=jnp.int32)))
    gz_img = gz_img.reshape(TOKENS, E)
    gp_img = normal_back(z_img, gz_img, r_img)
    gp_txt = normal_back(z_txt, gz_txt, r_txt)
    grad_image_features = jnp.dot(gp_img, image_proj.T, preferred_element_type=jnp.float32)
    grad_text_features = jnp.dot(gp_txt, text_proj.T, preferred_element_type=jnp.float32)
    grad_image_proj = jnp.dot(image_features.T, gp_img, preferred_element_type=jnp.float32)
    grad_text_proj = jnp.dot(text_features.T, gp_txt, preferred_element_type=jnp.float32)
    return (grad_image_features, grad_text_features, grad_image_proj, grad_text_proj)
```

```python
import jax
import jax.numpy as jnp
from jax import lax
from jax.sharding import Mesh, PartitionSpec as P

AXES = ("z", "xl", "y", "xh", "c")
SIZES = (8, 2, 4, 2, 2)
DP = ("z", "xl", "y")
MP = ("xh", "c")
PLANE = ("xl", "y", "xh")
BF = jnp.bfloat16
F32 = jnp.float32


def a2a(x, axes):
    return lax.all_to_all(x, axes, 0, 0, tiled=True)


def swap_core(x):
    return lax.ppermute(x, "c", [(0, 1), (1, 0)])


def rows_from_slices(pair):
    n = pair.shape[1] // 4
    parts = a2a(pair.reshape(2, 4, n, 288).transpose(1, 0, 2, 3), MP)
    return parts.transpose(1, 2, 0, 3).reshape(2, n, 1152)


def slices_from_rows(pair):
    n = pair.shape[1]
    parts = a2a(pair.reshape(2, n, 4, 288).transpose(2, 0, 1, 3), MP)
    return parts.transpose(1, 0, 2, 3).reshape(2, 4 * n, 288)


def shards(image_features, text_features, image_proj, text_proj, log_scale, bias):
    zi = lax.axis_index("z")
    ci = lax.axis_index("c")
    xl, y, xh = lax.axis_index("xl"), lax.axis_index("y"), lax.axis_index("xh")
    p_img = jnp.dot(image_features, image_proj, preferred_element_type=F32)
    p_txt = jnp.dot(text_features, text_proj, preferred_element_type=F32)
    own = rows_from_slices(jnp.stack([p_img, p_txt]).astype(BF)).astype(F32)
    r = lax.rsqrt(jnp.sum(own * own, axis=2, keepdims=True) + 1e-06)
    z = (own * r).astype(BF)
    z_img, z_txt = z[0], z[1]
    r_img, r_txt = r[0], r[1]

    txt_own = a2a(jnp.broadcast_to(z_txt[None], (8, 40, 1152)), ("z",)).reshape(320, 1152)
    img = a2a(jnp.broadcast_to(z_img[None], (16, 40, 1152)), PLANE).reshape(640, 1152)
    txt_oth = swap_core(txt_own)

    scale = jnp.exp(log_scale[0])
    offset = bias[0]
    place = (xl * 4 + y) * 2 + xh
    row_ids = jnp.arange(640, dtype=jnp.int32)[:, None] - place * 40
    col_ids = jnp.arange(320, dtype=jnp.int32)[None, :] - zi * 40
    diag = (row_ids == col_ids) & (row_ids >= 0) & (row_ids < 40)

    def coefs(txt, mask):
        d = jnp.einsum("re,ce->rc", img, txt, preferred_element_type=F32)
        logits = scale * d + offset
        if mask is None:
            return (scale * jax.nn.sigmoid(logits)).astype(BF)
        sign = jnp.where(mask, F32(1.0), F32(-1.0))
        return (-sign * jax.nn.sigmoid(-sign * logits) * scale).astype(BF)

    coef_oth = coefs(txt_oth, None)
    coef_own = coefs(txt_own, diag)
    t_oth = jnp.einsum("rc,re->ce", coef_oth, img, preferred_element_type=F32).astype(BF)
    t_got = swap_core(t_oth)
    t_own = jnp.einsum("rc,re->ce", coef_own, img, preferred_element_type=F32)
    t_sum = (t_own + t_got.astype(F32)).astype(BF).reshape(8, 40, 1152)
    g_img = (
        jnp.dot(coef_own, txt_own, preferred_element_type=F32)
        + jnp.dot(coef_oth, txt_oth, preferred_element_type=F32)
    ).astype(BF).reshape(16, 40, 1152)
    gz_txt = jnp.sum(a2a(t_sum, ("z",)).astype(F32), axis=0)
    gz_img = jnp.sum(a2a(g_img, PLANE).astype(F32), axis=0)

    gz = jnp.stack([gz_img, gz_txt])
    values = z.astype(F32)
    inner = jnp.sum(values * gz, axis=2, keepdims=True)
    gp_rows = (r * (gz - values * inner)).astype(BF)
    gp = slices_from_rows(gp_rows)
    gp_img, gp_txt = gp[0], gp[1]

    w_img = jnp.einsum("rd,re->de", image_features, gp_img, preferred_element_type=F32)
    w_txt = jnp.einsum("rd,re->de", text_features, gp_txt, preferred_element_type=F32)
    w = jnp.stack([w_img, w_txt]).astype(BF).reshape(2, 8, 8, 18, 288)
    w = w.transpose(2, 0, 1, 3, 4).reshape(8, 2 * 144, 288)
    w = jnp.sum(a2a(w, ("xl", "y")).astype(F32), axis=0).astype(BF)
    w = w.reshape(2, 8, 18, 288).transpose(1, 0, 2, 3)
    w = jnp.sum(a2a(w, ("z",)).astype(F32), axis=0)

    f_img = jnp.einsum("re,de->rd", gp_img, image_proj, preferred_element_type=F32)
    f_txt = jnp.einsum("re,de->rd", gp_txt, text_proj, preferred_element_type=F32)
    f = jnp.stack([f_img, f_txt]).astype(BF).reshape(2, 160, 4, 288).transpose(2, 0, 1, 3)
    f = jnp.sum(a2a(f, MP).astype(F32), axis=0)
    return f[0], f[1], w[0], w[1]


def solution(mesh):
    fine = Mesh(mesh.devices.reshape(SIZES), AXES)
    in_specs = (P(DP, None), P(DP, None), P(None, MP), P(None, MP), P(), P())
    out_specs = (P(DP, MP), P(DP, MP), P(DP, MP), P(DP, MP))
    return jax.shard_map(shards, mesh=fine, in_specs=in_specs, out_specs=out_specs, check_vma=False)
```

```python
import jax
import jax.numpy as jnp
from jax import lax
from jax.sharding import Mesh, PartitionSpec as P

AXES = ("z", "xl", "y", "xh", "c")
SIZES = (8, 2, 4, 2, 2)
DP = ("z", "xl", "y")
MP = ("xh", "c")
PLANE = ("xl", "y", "xh")
BF = jnp.bfloat16
F32 = jnp.float32


def a2a(x, axes):
    return lax.all_to_all(x, axes, 0, 0, tiled=True)


def swap_core(x):
    return lax.ppermute(x, "c", [(0, 1), (1, 0)])


def shift(x, axis, size, step):
    return lax.ppermute(x, axis, [(i, (i + step) % size) for i in range(size)])


def mp_shift(x, dx, dc):
    pairs = [(a * 2 + b, (a ^ dx) * 2 + (b ^ dc)) for a in range(2) for b in range(2)]
    return lax.ppermute(x, MP, pairs)


def rows_from_slices(pair):
    n = pair.shape[1] // 4
    parts = a2a(pair.reshape(2, 4, n, 288).transpose(1, 0, 2, 3), MP)
    return parts.transpose(1, 2, 0, 3).reshape(2, n, 1152)


def slices_from_rows(pair):
    n = pair.shape[1]
    parts = a2a(pair.reshape(2, n, 4, 288).transpose(2, 0, 1, 3), MP)
    return parts.transpose(1, 0, 2, 3).reshape(2, 4 * n, 288)


def shards(image_features, text_features, image_proj, text_proj, log_scale, bias):
    xl, y, xh, c = (lax.axis_index(a) for a in AXES[1:])
    p_img = jnp.dot(image_features, image_proj, preferred_element_type=F32)
    p_txt = jnp.dot(text_features, text_proj, preferred_element_type=F32)
    own = rows_from_slices(jnp.stack([p_img, p_txt]))
    r = lax.rsqrt(jnp.sum(own * own, axis=2, keepdims=True) + 1e-06)
    z = (own * r).astype(BF)
    z_img, z_txt = z[0], z[1]
    r_img, r_txt = r[0], r[1]

    img = a2a(jnp.broadcast_to(z_img[None], (16, 40, 1152)), PLANE).reshape(640, 1152)
    txt_own = jnp.concatenate([z_txt] + [shift(z_txt, "z", 8, d) for d in range(1, 8)])
    txt_oth = swap_core(txt_own)

    scale = jnp.exp(log_scale[0])
    offset = bias[0]
    place = (xl * 4 + y) * 2 + xh
    row_ids = jnp.arange(640, dtype=jnp.int32)[:, None] - place * 40
    col_ids = jnp.arange(320, dtype=jnp.int32)[None, :]
    diag = (row_ids == col_ids) & (row_ids >= 0) & (row_ids < 40)

    def coefs(txt, mask):
        d = jnp.einsum("re,ce->rc", img, txt, preferred_element_type=F32)
        logits = scale * d + offset
        if mask is None:
            return (scale * jax.nn.sigmoid(logits)).astype(BF)
        sign = jnp.where(mask, F32(1.0), F32(-1.0))
        return (-sign * jax.nn.sigmoid(-sign * logits) * scale).astype(BF)

    coef_oth = coefs(txt_oth, None)
    coef_own = coefs(txt_own, diag)
    t_oth = jnp.einsum("rc,re->ce", coef_oth, img, preferred_element_type=F32).astype(BF)
    t_got = swap_core(t_oth)
    t_own = jnp.einsum("rc,re->ce", coef_own, img, preferred_element_type=F32)
    t_sum = t_own + t_got.astype(F32)
    t_out = t_sum[40:].astype(BF)
    gz_txt = t_sum[:40]
    for d in range(1, 8):
        gz_txt = gz_txt + shift(t_out[40 * d - 40 : 40 * d], "z", 8, -d).astype(F32)
    g_img = (
        jnp.dot(coef_own, txt_own, preferred_element_type=F32)
        + jnp.dot(coef_oth, txt_oth, preferred_element_type=F32)
    ).astype(BF).reshape(16, 40, 1152)
    gz_img = jnp.sum(a2a(g_img, PLANE).astype(F32), axis=0)

    gz = jnp.stack([gz_img, gz_txt])
    values = z.astype(F32)
    inner = jnp.sum(values * gz, axis=2, keepdims=True)
    gp_rows = (r * (gz - values * inner)).astype(BF)
    gp = slices_from_rows(gp_rows)
    gp_img, gp_txt = gp[0], gp[1]

    w_img = jnp.einsum("rd,re->de", image_features, gp_img, preferred_element_type=F32)
    w_txt = jnp.einsum("rd,re->de", text_features, gp_txt, preferred_element_type=F32)
    w = jnp.stack([w_img, w_txt]).astype(BF).reshape(2, 8, 8, 18, 288)
    w = w.transpose(2, 0, 1, 3, 4).reshape(8, 2 * 144, 288)
    w = jnp.sum(a2a(w, ("xl", "y")).astype(F32), axis=0).astype(BF)
    w = w.reshape(2, 8, 18, 288).transpose(1, 0, 2, 3)
    w = jnp.sum(a2a(w, ("z",)).astype(F32), axis=0)

    f_img = jnp.einsum("re,de->rd", gp_img, image_proj, preferred_element_type=F32)
    f_txt = jnp.einsum("re,de->rd", gp_txt, text_proj, preferred_element_type=F32)
    f = jnp.stack([f_img, f_txt]).reshape(2, 160, 4, 288).transpose(2, 0, 1, 3)
    me = xh * 2 + c
    total = lax.dynamic_index_in_dim(f, me, 0, keepdims=False)
    f = f.astype(BF)
    for dx, dc in ((0, 1), (1, 0), (1, 1)):
        other = lax.dynamic_index_in_dim(f, (xh ^ dx) * 2 + (c ^ dc), 0, keepdims=False)
        total = total + mp_shift(other, dx, dc).astype(F32)
    f = total
    return f[0], f[1], w[0], w[1]


def solution(mesh):
    fine = Mesh(mesh.devices.reshape(SIZES), AXES)
    in_specs = (P(DP, None), P(DP, None), P(None, MP), P(None, MP), P(), P())
    out_specs = (P(DP, MP), P(DP, MP), P(DP, MP), P(DP, MP))
    return jax.shard_map(shards, mesh=fine, in_specs=in_specs, out_specs=out_specs, check_vma=False)
```

```python
import jax
import jax.numpy as jnp
from jax import lax
from jax.sharding import Mesh, PartitionSpec as P

AXES = ("z", "xl", "y", "xh", "c")
SIZES = (8, 2, 4, 2, 2)
DP = ("z", "xl", "y")
MP = ("xh", "c")
PLANE = ("xl", "y", "xh")
BF = jnp.bfloat16
F32 = jnp.float32


def a2a(x, axes):
    return lax.all_to_all(x, axes, 0, 0, tiled=True)


def swap_core(x):
    return lax.ppermute(x, "c", [(0, 1), (1, 0)])


def shift(x, axis, size, step):
    return lax.ppermute(x, axis, [(i, (i + step) % size) for i in range(size)])


def mp_shift(x, dx, dc):
    pairs = [(a * 2 + b, (a ^ dx) * 2 + (b ^ dc)) for a in range(2) for b in range(2)]
    return lax.ppermute(x, MP, pairs)


def rows_from_slices(pair, xh, c):
    quarters = pair.reshape(2, 2, 2, 40, 288)
    got = {}
    for dx in range(2):
        for dc in range(2):
            to = lax.dynamic_index_in_dim(quarters, xh ^ dx, 1, keepdims=False)
            to = lax.dynamic_index_in_dim(to, c ^ dc, 1, keepdims=False)
            got[dx, dc] = mp_shift(to, dx, dc) if dx or dc else to
    parts = []
    for a in range(2):
        for b in range(2):
            near = jnp.where(c == b, got[0, 0], got[0, 1])
            far = jnp.where(c == b, got[1, 0], got[1, 1])
            parts.append(jnp.where(xh == a, near, far))
    return jnp.concatenate(parts, axis=2)


def shards(image_features, text_features, image_proj, text_proj, log_scale, bias):
    zi = lax.axis_index("z")
    xl, y, xh, c = (lax.axis_index(a) for a in AXES[1:])
    both = jnp.concatenate(
        [
            feats.reshape(160, 8, 8, 18).transpose(2, 0, 1, 3).reshape(8, 160, 144)
            for feats in (image_features, text_features)
        ],
        axis=2,
    )
    plane_features = a2a(both, ("xl", "y")).reshape(1280, 288)
    p_img = jnp.dot(image_features, image_proj, preferred_element_type=F32)
    p_txt = jnp.dot(text_features, text_proj, preferred_element_type=F32)
    own = rows_from_slices(jnp.stack([p_img, p_txt]), xh, c)
    r = lax.rsqrt(jnp.sum(own * own, axis=2, keepdims=True) + 1e-06)
    z = (own * r).astype(BF)
    z, plane_features = lax.optimization_barrier((z, plane_features))
    z_img, z_txt = z[0], z[1]
    r_img, r_txt = r[0], r[1]

    img = a2a(jnp.broadcast_to(z_img[None], (16, 40, 1152)), PLANE).reshape(640, 1152)
    txt_own = lax.all_gather(z_txt, "z", axis=0, tiled=True)
    txt_oth = swap_core(txt_own)

    scale = jnp.exp(log_scale[0])
    offset = bias[0]
    place = (xl * 4 + y) * 2 + xh
    row_ids = jnp.arange(640, dtype=jnp.int32)[:, None] - place * 40
    col_ids = jnp.arange(320, dtype=jnp.int32)[None, :] - zi * 40
    diag = (row_ids == col_ids) & (row_ids >= 0) & (row_ids < 40)

    def coefs(txt, mask):
        d = jnp.einsum("re,ce->rc", img, txt, preferred_element_type=F32)
        logits = scale * d + offset
        if mask is None:
            return (scale * jax.nn.sigmoid(logits)).astype(BF)
        sign = jnp.where(mask, F32(1.0), F32(-1.0))
        return (-sign * jax.nn.sigmoid(-sign * logits) * scale).astype(BF)

    coef_oth = coefs(txt_oth, None)
    coef_own = coefs(txt_own, diag)
    t_oth = jnp.einsum("rc,re->ce", coef_oth, img, preferred_element_type=F32).astype(BF)
    t_got = swap_core(t_oth)
    t_own = jnp.einsum("rc,re->ce", coef_own, img, preferred_element_type=F32)
    t_sum = t_own + t_got.astype(F32)
    t_sum = t_sum.reshape(8, 40, 1152)
    gz_txt = lax.dynamic_index_in_dim(t_sum, zi, 0, keepdims=False)
    t_out = t_sum.astype(BF)
    for d in range(1, 8):
        piece = lax.dynamic_index_in_dim(t_out, (zi + d) % 8, 0, keepdims=False)
        gz_txt = gz_txt + shift(piece, "z", 8, d).astype(F32)
    g_img = (
        jnp.dot(coef_own, txt_own, preferred_element_type=F32)
        + jnp.dot(coef_oth, txt_oth, preferred_element_type=F32)
    ).astype(BF).reshape(16, 40, 1152)
    gz_img = jnp.sum(a2a(g_img, PLANE).astype(F32), axis=0)

    gz = jnp.stack([gz_img, gz_txt])
    values = z.astype(F32)
    inner = jnp.sum(values * gz, axis=2, keepdims=True)
    gp_rows = (r * (gz - values * inner)).astype(BF)
    cut = gp_rows.reshape(2, 40, 4, 288).transpose(2, 0, 1, 3)
    rest = jnp.concatenate([cut[:, 0, :, 256:], cut[:, 1, :, 256:], jnp.zeros((4, 40, 64), BF)], axis=2)
    piece = jnp.concatenate(
        [cut[:, :, :, :128].reshape(4, 80, 128), cut[:, :, :, 128:256].reshape(4, 80, 128), rest], axis=1
    )
    got = a2a(jnp.broadcast_to(piece[None], (8, 4, 200, 128)).reshape(32, 200, 128), ("xl", "y", "xh", "c"))
    cols = [got[:, 40 * i : 40 * i + 40].reshape(1280, 128) for i in (0, 2, 1, 3, 4)]
    w = jnp.einsum("rd,re->de", plane_features, jnp.concatenate(cols, axis=1), preferred_element_type=F32)
    w = jnp.stack([jnp.concatenate([w[:144, :256], w[:144, 512:544]], axis=1), jnp.concatenate([w[144:, 256:512], w[144:, 544:576]], axis=1)])
    w = w.astype(BF).reshape(2, 8, 18, 288).transpose(1, 0, 2, 3)
    w = jnp.sum(a2a(w, ("z",)).astype(F32), axis=0)

    mine = lax.dynamic_slice_in_dim(got, (xl * 4 + y) * 4, 4, 0)
    mine = [mine[:, 40 * i : 40 * i + 40].reshape(160, 128) for i in range(5)]
    gp_img = jnp.concatenate([mine[0], mine[2], mine[4][:, :32]], axis=1)
    gp_txt = jnp.concatenate([mine[1], mine[3], mine[4][:, 32:64]], axis=1)
    f_img = jnp.einsum("re,de->rd", gp_img, image_proj, preferred_element_type=F32)
    f_txt = jnp.einsum("re,de->rd", gp_txt, text_proj, preferred_element_type=F32)
    f = jnp.stack([f_img, f_txt]).reshape(2, 160, 4, 288).transpose(2, 0, 1, 3)
    me = xh * 2 + c
    total = lax.dynamic_index_in_dim(f, me, 0, keepdims=False)
    f = f.astype(BF)
    for dx, dc in ((0, 1), (1, 0), (1, 1)):
        other = lax.dynamic_index_in_dim(f, (xh ^ dx) * 2 + (c ^ dc), 0, keepdims=False)
        total = total + mp_shift(other, dx, dc).astype(F32)
    f = total
    return f[0], f[1], w[0], w[1]


def solution(mesh):
    fine = Mesh(mesh.devices.reshape(SIZES), AXES)
    in_specs = (P(DP, None), P(DP, None), P(None, MP), P(None, MP), P(), P())
    out_specs = (P(DP, MP), P(DP, MP), P(DP, MP), P(DP, MP))
    return jax.shard_map(shards, mesh=fine, in_specs=in_specs, out_specs=out_specs, check_vma=False)
```

```python
import jax
import jax.numpy as jnp
from jax import lax
from jax.sharding import Mesh, PartitionSpec as P

AXES = ("z", "xl", "y", "xh", "c")
SIZES = (8, 2, 4, 2, 2)
DP = ("z", "xl", "y")
MP = ("xh", "c")
PLANE = ("xl", "y", "xh")
BF = jnp.bfloat16
F32 = jnp.float32


def a2a(x, axes):
    return lax.all_to_all(x, axes, 0, 0, tiled=True)


def swap_core(x):
    return lax.ppermute(x, "c", [(0, 1), (1, 0)])


def shift(x, axis, size, step):
    return lax.ppermute(x, axis, [(i, (i + step) % size) for i in range(size)])


def mp_shift(x, dx, dc):
    pairs = [(a * 2 + b, (a ^ dx) * 2 + (b ^ dc)) for a in range(2) for b in range(2)]
    return lax.ppermute(x, MP, pairs)


def rows_from_slices(pair, xh, c):
    quarters = pair.reshape(2, 2, 2, 40, 288)
    got = {}
    for dx in range(2):
        for dc in range(2):
            to = lax.dynamic_index_in_dim(quarters, xh ^ dx, 1, keepdims=False)
            to = lax.dynamic_index_in_dim(to, c ^ dc, 1, keepdims=False)
            got[dx, dc] = mp_shift(to, dx, dc) if dx or dc else to
    parts = []
    for a in range(2):
        for b in range(2):
            near = jnp.where(c == b, got[0, 0], got[0, 1])
            far = jnp.where(c == b, got[1, 0], got[1, 1])
            parts.append(jnp.where(xh == a, near, far))
    return jnp.concatenate(parts, axis=2)


def shards(image_features, text_features, image_proj, text_proj, log_scale, bias):
    xl, y, xh, c = (lax.axis_index(a) for a in AXES[1:])
    p_img = jnp.dot(image_features, image_proj, preferred_element_type=F32)
    p_txt = jnp.dot(text_features, text_proj, preferred_element_type=F32)
    own = rows_from_slices(jnp.stack([p_img, p_txt]), xh, c)
    r = lax.rsqrt(jnp.sum(own * own, axis=2, keepdims=True) + 1e-06)
    z = (own * r).astype(BF)
    z_img, z_txt = z[0], z[1]
    r_img, r_txt = r[0], r[1]

    img = jnp.broadcast_to(z_img[None], (16, 40, 1152))
    img, z_near = lax.optimization_barrier((img, z_txt))
    img = a2a(img, PLANE).reshape(640, 1152)
    up, down = [z_near], [z_near]
    for d in range(3):
        up.append(shift(up[-1], "z", 8, 1))
        down.append(shift(down[-1], "z", 8, -1))
    up.append(shift(up[-1], "z", 8, 1))
    txt_own = jnp.concatenate(up + down[:0:-1])

    feats = [
        f.reshape(160, 8, 2, 4, 18).transpose(2, 0, 3, 1, 4).reshape(2, 160, 576)
        for f in lax.optimization_barrier((image_features, text_features, down[2]))[:2]
    ]
    feats = jnp.concatenate(feats, axis=2)
    keep = lax.dynamic_index_in_dim(feats, xl, 0, keepdims=False)
    come = lax.ppermute(lax.dynamic_index_in_dim(feats, 1 - xl, 0, keepdims=False), "xl", [(0, 1), (1, 0)])
    keep, come, img = lax.optimization_barrier((keep, come, img))
    feats = jnp.concatenate([jnp.where(xl == 0, keep, come), jnp.where(xl == 0, come, keep)])

    txt_oth = swap_core(txt_own)

    scale = jnp.exp(log_scale[0])
    offset = bias[0]
    place = (xl * 4 + y) * 2 + xh
    row_ids = jnp.arange(640, dtype=jnp.int32)[:, None] - place * 40
    col_ids = jnp.arange(320, dtype=jnp.int32)[None, :]
    diag = (row_ids == col_ids) & (row_ids >= 0) & (row_ids < 40)

    def coefs(txt, mask):
        d = jnp.einsum("re,ce->rc", img, txt, preferred_element_type=F32)
        logits = scale * d + offset
        if mask is None:
            return (scale * jax.nn.sigmoid(logits)).astype(BF)
        sign = jnp.where(mask, F32(1.0), F32(-1.0))
        return (-sign * jax.nn.sigmoid(-sign * logits) * scale).astype(BF)

    coef_oth = coefs(txt_oth, None)
    coef_own = coefs(txt_own, diag)
    t_oth = jnp.einsum("rc,re->ce", coef_oth, img, preferred_element_type=F32).astype(BF)
    t_got = swap_core(t_oth)
    t_own = jnp.einsum("rc,re->ce", coef_own, img, preferred_element_type=F32)
    t_sum = t_own + t_got.astype(F32)
    blocks = [t_sum[40 * d : 40 * d + 40] for d in range(8)]
    up, down = blocks[4], blocks[3]
    for d in range(1, 5):
        up = shift(up.astype(BF), "z", 8, 1).astype(F32) + blocks[(4 + d) % 8]
        if d < 3:
            down = shift(down.astype(BF), "z", 8, -1).astype(F32) + blocks[3 - d]
    gz_txt = up + shift(down.astype(BF), "z", 8, -1).astype(F32)
    g_img = (
        jnp.dot(coef_own, txt_own, preferred_element_type=F32)
        + jnp.dot(coef_oth, txt_oth, preferred_element_type=F32)
    ).astype(BF).reshape(16, 40, 1152)
    gz_img = jnp.sum(a2a(g_img, PLANE).astype(F32), axis=0)

    gz = jnp.stack([gz_img, gz_txt])
    values = z.astype(F32)
    inner = jnp.sum(values * gz, axis=2, keepdims=True)
    gp_rows = (r * (gz - values * inner)).astype(BF)
    cut = gp_rows.reshape(2, 40, 4, 288).transpose(2, 0, 1, 3)
    rest = jnp.concatenate([cut[:, 0, :, 256:], cut[:, 1, :, 256:], jnp.zeros((4, 40, 64), BF)], axis=2)
    piece = jnp.concatenate(
        [cut[:, :, :, :128].reshape(4, 80, 128), cut[:, :, :, 128:256].reshape(4, 80, 128), rest], axis=1
    )
    got = a2a(jnp.broadcast_to(piece[None], (2, 4, 200, 128)).reshape(8, 200, 128), ("xl", "xh", "c"))
    a_img, a_txt, b_img, b_txt, rest = (got[:, 40 * i : 40 * i + 40].reshape(320, 128) for i in range(5))

    def rows_dot(x, g):
        return jnp.einsum("rd,re->de", x, g, preferred_element_type=F32)

    lane = jnp.arange(128, dtype=jnp.int32)[None, :]
    rest_img = jnp.where(lane < 32, rest, jnp.zeros_like(rest))
    rest_txt = jnp.where(lane < 32, jnp.zeros_like(rest), rest)
    fi, ft = feats[:, :576], feats[:, 576:]
    w = jnp.concatenate(
        [
            rows_dot(fi, jnp.concatenate([a_img, b_img], axis=1)),
            rows_dot(ft, jnp.concatenate([a_txt, b_txt], axis=1)),
            rows_dot(fi, rest_img) + rows_dot(ft, rest_txt),
        ],
        axis=1,
    ).reshape(4, 144, 640)
    up = lax.dynamic_index_in_dim(w, (y + 2) % 4, 0, keepdims=False).astype(BF)
    down = lax.dynamic_index_in_dim(w, (y + 3) % 4, 0, keepdims=False).astype(BF)
    up = shift(up, "y", 4, 1).astype(F32) + lax.dynamic_index_in_dim(w, (y + 1) % 4, 0, keepdims=False)
    w = lax.dynamic_index_in_dim(w, y, 0, keepdims=False) + shift(down, "y", 4, -1).astype(F32)
    w = w + shift(up.astype(BF), "y", 4, 1).astype(F32)
    w = jnp.sum(a2a(w.astype(BF).reshape(8, 18, 640), ("z",)).astype(F32), axis=0)
    w_img = jnp.concatenate([w[:, :256], w[:, 512:544]], axis=1)
    w_txt = jnp.concatenate([w[:, 256:512], w[:, 544:576]], axis=1)

    mine = lax.dynamic_slice_in_dim(got, xl * 4, 4, 0)
    mine = [mine[:, 40 * i : 40 * i + 40].reshape(160, 128) for i in range(5)]
    gp_img = jnp.concatenate([mine[0], mine[2], mine[4][:, :32]], axis=1)
    gp_txt = jnp.concatenate([mine[1], mine[3], mine[4][:, 32:64]], axis=1)

    def feature_part(to):
        out = [
            jnp.einsum("re,de->rd", g, lax.dynamic_slice_in_dim(p, to * 288, 288, 0), preferred_element_type=F32)
            for g, p in ((gp_img, image_proj), (gp_txt, text_proj))
        ]
        return jnp.stack(out)

    f = feature_part(xh * 2 + c)
    for dx, dc in ((0, 1), (1, 0), (1, 1)):
        other = feature_part((xh ^ dx) * 2 + (c ^ dc)).astype(BF)
        f = f + mp_shift(other, dx, dc).astype(F32)
    return f[0], f[1], w_img, w_txt


def solution(mesh):
    fine = Mesh(mesh.devices.reshape(SIZES), AXES)
    in_specs = (P(DP, None), P(DP, None), P(None, MP), P(None, MP), P(), P())
    out_specs = (P(DP, MP), P(DP, MP), P(DP, MP), P(DP, MP))
    return jax.shard_map(shards, mesh=fine, in_specs=in_specs, out_specs=out_specs, check_vma=False)
```

```python
import jax
import jax.numpy as jnp
from jax import lax
from jax.sharding import Mesh, PartitionSpec as P

AXES = ("z", "xl", "y", "xh", "c")
SIZES = (8, 2, 4, 2, 2)
DP = ("z", "xl", "y")
MP = ("xh", "c")
PLANE = ("xl", "y", "xh")
BF = jnp.bfloat16
F32 = jnp.float32


def a2a(x, axes):
    return lax.all_to_all(x, axes, 0, 0, tiled=True)


def swap_core(x):
    return lax.ppermute(x, "c", [(0, 1), (1, 0)])


def shift(x, axis, size, step):
    return lax.ppermute(x, axis, [(i, (i + step) % size) for i in range(size)])


def mp_shift(x, dx, dc):
    pairs = [(a * 2 + b, (a ^ dx) * 2 + (b ^ dc)) for a in range(2) for b in range(2)]
    return lax.ppermute(x, MP, pairs)


def rows_from_slices(pair, xh, c):
    quarters = pair.reshape(2, 2, 2, 40, 288)
    got = {}
    for dx in range(2):
        for dc in range(2):
            to = lax.dynamic_index_in_dim(quarters, xh ^ dx, 1, keepdims=False)
            to = lax.dynamic_index_in_dim(to, c ^ dc, 1, keepdims=False)
            got[dx, dc] = mp_shift(to, dx, dc) if dx or dc else to
    parts = []
    for a in range(2):
        for b in range(2):
            near = jnp.where(c == b, got[0, 0], got[0, 1])
            far = jnp.where(c == b, got[1, 0], got[1, 1])
            parts.append(jnp.where(xh == a, near, far))
    return jnp.concatenate(parts, axis=2)


def shards(image_features, text_features, image_proj, text_proj, log_scale, bias):
    xl, y, xh, c = (lax.axis_index(a) for a in AXES[1:])
    p_img = jnp.dot(image_features, image_proj, preferred_element_type=F32)
    p_txt = jnp.dot(text_features, text_proj, preferred_element_type=F32)
    own = rows_from_slices(jnp.stack([p_img, p_txt]), xh, c)
    r = lax.rsqrt(jnp.sum(own * own, axis=2, keepdims=True) + 1e-06)
    z = (own * r).astype(BF)
    z_img, z_txt = z[0], z[1]
    r_img, r_txt = r[0], r[1]

    img = jnp.broadcast_to(z_img[None], (16, 40, 1152))
    img, z_near = lax.optimization_barrier((img, z_txt))
    img = a2a(img, PLANE).reshape(640, 1152)
    up, down = [z_near], [z_near]
    for d in range(3):
        up.append(shift(up[-1], "z", 8, 1))
        down.append(shift(down[-1], "z", 8, -1))
    up.append(shift(up[-1], "z", 8, 1))
    txt_own = jnp.concatenate(up + down[:0:-1])

    stacked = jnp.concatenate(lax.optimization_barrier((image_features, text_features, down[2]))[:2])
    col = jnp.arange(576, dtype=jnp.int32)
    source = (col % 144) // 18 * 144 + col // 144 * 18 + col % 18

    def pick(half):
        chosen = jnp.arange(1152, dtype=jnp.int32)[:, None] == (source + 72 * half)[None, :]
        return jnp.dot(stacked, chosen.astype(BF), preferred_element_type=F32).astype(BF)

    keep = pick(xl)
    come = lax.ppermute(pick(1 - xl), "xl", [(0, 1), (1, 0)])
    keep, come, img = lax.optimization_barrier((keep, come, img))
    first, second = jnp.where(xl == 0, keep, come), jnp.where(xl == 0, come, keep)
    fi = jnp.concatenate([first[:160], second[:160]])
    ft = jnp.concatenate([first[160:], second[160:]])

    txt_oth = swap_core(txt_own)

    scale = jnp.exp(log_scale[0])
    offset = bias[0]
    place = (xl * 4 + y) * 2 + xh
    row_ids = jnp.arange(640, dtype=jnp.int32)[:, None] - place * 40
    col_ids = jnp.arange(320, dtype=jnp.int32)[None, :]
    diag = (row_ids == col_ids) & (row_ids >= 0) & (row_ids < 40)

    def coefs(txt, mask):
        d = jnp.einsum("re,ce->rc", img, txt, preferred_element_type=F32)
        logits = scale * d + offset
        if mask is None:
            return (scale * jax.nn.sigmoid(logits)).astype(BF)
        sign = jnp.where(mask, F32(1.0), F32(-1.0))
        return (-sign * jax.nn.sigmoid(-sign * logits) * scale).astype(BF)

    coef_oth = coefs(txt_oth, None)
    coef_own = coefs(txt_own, diag)
    t_oth = jnp.einsum("rc,re->ce", coef_oth, img, preferred_element_type=F32).astype(BF)
    t_got = swap_core(t_oth)
    t_own = jnp.einsum("rc,re->ce", coef_own, img, preferred_element_type=F32)
    t_sum = t_own + t_got.astype(F32)
    blocks = [t_sum[40 * d : 40 * d + 40] for d in range(8)]
    up, down = blocks[4], blocks[3]
    for d in range(1, 5):
        up = shift(up.astype(BF), "z", 8, 1).astype(F32) + blocks[(4 + d) % 8]
        if d < 3:
            down = shift(down.astype(BF), "z", 8, -1).astype(F32) + blocks[3 - d]
    gz_txt = up + shift(down.astype(BF), "z", 8, -1).astype(F32)
    g_img = (
        jnp.dot(coef_own, txt_own, preferred_element_type=F32)
        + jnp.dot(coef_oth, txt_oth, preferred_element_type=F32)
    ).astype(BF).reshape(16, 40, 1152)
    gz_img = jnp.sum(a2a(g_img, PLANE).astype(F32), axis=0)

    gz = jnp.stack([gz_img, gz_txt])
    values = z.astype(F32)
    inner = jnp.sum(values * gz, axis=2, keepdims=True)
    gp_rows = (r * (gz - values * inner)).astype(BF)
    cut = gp_rows.reshape(2, 40, 4, 288).transpose(2, 0, 1, 3)
    rest = jnp.concatenate([cut[:, 0, :, 256:], cut[:, 1, :, 256:], jnp.zeros((4, 40, 64), BF)], axis=2)
    piece = jnp.concatenate(
        [cut[:, :, :, :128].reshape(4, 80, 128), cut[:, :, :, 128:256].reshape(4, 80, 128), rest], axis=1
    )
    got = a2a(jnp.broadcast_to(piece[None], (2, 4, 200, 128)).reshape(8, 200, 128), ("xl", "xh", "c"))
    a_img, a_txt, b_img, b_txt, rest = (got[:, 40 * i : 40 * i + 40].reshape(320, 128) for i in range(5))

    def rows_dot(x, g):
        return jnp.einsum("rd,re->de", x, g, preferred_element_type=F32)

    lane = jnp.arange(128, dtype=jnp.int32)[None, :]
    rest_img = jnp.where(lane < 32, rest, jnp.zeros_like(rest))
    rest_txt = jnp.where(lane < 32, jnp.zeros_like(rest), rest)
    w = jnp.concatenate(
        [
            rows_dot(fi, jnp.concatenate([a_img, b_img], axis=1)),
            rows_dot(ft, jnp.concatenate([a_txt, b_txt], axis=1)),
            rows_dot(fi, rest_img) + rows_dot(ft, rest_txt),
        ],
        axis=1,
    ).reshape(4, 144, 640)
    up = lax.dynamic_index_in_dim(w, (y + 2) % 4, 0, keepdims=False).astype(BF)
    down = lax.dynamic_index_in_dim(w, (y + 3) % 4, 0, keepdims=False).astype(BF)
    up, got = lax.optimization_barrier((shift(up, "y", 4, 1), got))
    up = up.astype(F32) + lax.dynamic_index_in_dim(w, (y + 1) % 4, 0, keepdims=False)
    w = lax.dynamic_index_in_dim(w, y, 0, keepdims=False) + shift(down, "y", 4, -1).astype(F32)
    w = w + shift(up.astype(BF), "y", 4, 1).astype(F32)
    w = jnp.sum(a2a(w.astype(BF).reshape(8, 18, 640), ("z",)).astype(F32), axis=0)
    w_img = jnp.concatenate([w[:, :256], w[:, 512:544]], axis=1)
    w_txt = jnp.concatenate([w[:, 256:512], w[:, 544:576]], axis=1)

    mine = lax.dynamic_slice_in_dim(got, xl * 4, 4, 0)
    mine = [mine[:, 40 * i : 40 * i + 40].reshape(160, 128) for i in range(5)]
    gp_img = jnp.concatenate([mine[0], mine[2], mine[4][:, :32]], axis=1)
    gp_txt = jnp.concatenate([mine[1], mine[3], mine[4][:, 32:64]], axis=1)

    def feature_part(to):
        out = [
            jnp.einsum("re,de->rd", g, lax.dynamic_slice_in_dim(p, to * 288, 288, 0), preferred_element_type=F32)
            for g, p in ((gp_img, image_proj), (gp_txt, text_proj))
        ]
        return jnp.stack(out)

    f = feature_part(xh * 2 + c)
    for dx, dc in ((0, 1), (1, 0), (1, 1)):
        other = feature_part((xh ^ dx) * 2 + (c ^ dc)).astype(BF)
        f = f + mp_shift(other, dx, dc).astype(F32)
    return f[0], f[1], w_img, w_txt


def solution(mesh):
    fine = Mesh(mesh.devices.reshape(SIZES), AXES)
    in_specs = (P(DP, None), P(DP, None), P(None, MP), P(None, MP), P(), P())
    out_specs = (P(DP, MP), P(DP, MP), P(DP, MP), P(DP, MP))
    return jax.shard_map(shards, mesh=fine, in_specs=in_specs, out_specs=out_specs, check_vma=False)
```

```python
import jax
import jax.numpy as jnp
from jax import lax
from jax.experimental import pallas as pl
from jax.experimental.pallas import tpu as pltpu
from jax.sharding import Mesh, PartitionSpec as P

AXES = ("z", "xl", "y", "xh", "c")
SIZES = (8, 2, 4, 2, 2)
DP = ("z", "xl", "y")
MP = ("xh", "c")
PLANE = ("xl", "y", "xh")
BF = jnp.bfloat16
F32 = jnp.float32


def a2a(x, axes):
    return lax.all_to_all(x, axes, 0, 0, tiled=True)


def swap_core(x):
    return lax.ppermute(x, "c", [(0, 1), (1, 0)])


def shift(x, axis, size, step):
    return lax.ppermute(x, axis, [(i, (i + step) % size) for i in range(size)])


def mp_shift(x, dx, dc):
    pairs = [(a * 2 + b, (a ^ dx) * 2 + (b ^ dc)) for a in range(2) for b in range(2)]
    return lax.ppermute(x, MP, pairs)


def rows_from_slices(pair, xh, c):
    quarters = pair.reshape(2, 2, 2, 40, 288)
    got = {}
    for dx in range(2):
        for dc in range(2):
            to = lax.dynamic_index_in_dim(quarters, xh ^ dx, 1, keepdims=False)
            to = lax.dynamic_index_in_dim(to, c ^ dc, 1, keepdims=False)
            got[dx, dc] = mp_shift(to, dx, dc) if dx or dc else to
    parts = []
    for a in range(2):
        for b in range(2):
            near = jnp.where(c == b, got[0, 0], got[0, 1])
            far = jnp.where(c == b, got[1, 0], got[1, 1])
            parts.append(jnp.where(xh == a, near, far))
    return jnp.concatenate(parts, axis=2)


def block_kernel(scalars, place, img_in, *refs):
    pieces, (t_oth, t_own, g_img, img, parts, texts, coef_t, img_sem, sems) = refs[:16], refs[16:]
    scale, offset = scalars[0], scalars[1]
    img_copy = pltpu.make_async_copy(img_in, img, img_sem)
    copies = [pltpu.make_async_copy(pieces[d], parts.at[d], sems.at[d]) for d in range(16)]
    for copy in copies:
        copy.start()
    img_copy.start()
    for d in range(8):
        copies[2 * d].wait()
        copies[2 * d + 1].wait()
        texts[80 * d : 80 * d + 80, :] = jnp.concatenate([parts[2 * d], parts[2 * d + 1]])
    img_copy.wait()
    first = place[0] * 40

    def images(i, _):
        at = pl.multiple_of(i * 128, 128)
        block = img[pl.ds(at, 128), :]
        dots = lax.dot_general(block, texts[...], (((1,), (1,)), ((), ())), preferred_element_type=F32)
        rows = lax.broadcasted_iota(jnp.int32, (128, 640), 0) + at - first
        cols = lax.broadcasted_iota(jnp.int32, (128, 640), 1) - 320
        sign = jnp.where((rows == cols) & (cols >= 0) & (cols < 40), F32(1.0), F32(-1.0))
        value = -sign * scale * jax.nn.sigmoid(-sign * (scale * dots + offset))
        coef_t[:, pl.ds(at, 128)] = value.T.astype(BF)
        value = value.astype(BF)
        g_img[pl.ds(at, 128), :] = jnp.dot(value, texts[...], preferred_element_type=F32).astype(BF)
        return 0

    lax.fori_loop(0, 5, images, 0)

    def others(j, _):
        at = pl.multiple_of(j * 160, 32)
        t_oth[pl.ds(at, 160), :] = jnp.dot(
            coef_t[pl.ds(at, 160), :], img[...], preferred_element_type=F32
        ).astype(BF)
        return 0

    lax.fori_loop(0, 2, others, 0)

    def owns(j, _):
        at = pl.multiple_of(j * 160, 32)
        t_own[pl.ds(at, 160), :] = jnp.dot(coef_t[pl.ds(320 + at, 160), :], img[...], preferred_element_type=F32)
        return 0

    lax.fori_loop(0, 2, owns, 0)


def block_grads(scalars, place, img, pieces):
    small = pl.BlockSpec(memory_space=pltpu.SMEM)
    large = pl.BlockSpec(memory_space=pl.ANY)
    vmem = pl.BlockSpec(memory_space=pltpu.VMEM)
    return pl.pallas_call(
        block_kernel,
        out_shape=[
            jax.ShapeDtypeStruct((320, 1152), BF),
            jax.ShapeDtypeStruct((320, 1152), F32),
            jax.ShapeDtypeStruct((640, 1152), BF),
        ],
        in_specs=[small, small] + [large] * 17,
        out_specs=[vmem] * 3,
        scratch_shapes=[
            pltpu.VMEM((640, 1152), BF),
            pltpu.VMEM((16, 40, 1152), BF),
            pltpu.VMEM((640, 1152), BF),
            pltpu.VMEM((640, 640), BF),
            pltpu.SemaphoreType.DMA,
            pltpu.SemaphoreType.DMA((16,)),
        ],
        compiler_params=pltpu.CompilerParams(vmem_limit_bytes=24 * 2**20),
        cost_estimate=pl.CostEstimate(flops=2900000000, bytes_accessed=8000000, transcendentals=400000),
    )(scalars, place, img, *pieces)


def shards(image_features, text_features, image_proj, text_proj, log_scale, bias):
    xl, y, xh, c = (lax.axis_index(a) for a in AXES[1:])
    p_img = jnp.dot(image_features, image_proj, preferred_element_type=F32)
    p_txt = jnp.dot(text_features, text_proj, preferred_element_type=F32)
    stacked = jnp.concatenate(lax.optimization_barrier((image_features, text_features, p_img, p_txt))[:2])
    col = jnp.arange(576, dtype=jnp.int32)
    source = (col % 144) // 18 * 144 + col // 144 * 18 + col % 18

    def pick(half):
        chosen = jnp.arange(1152, dtype=jnp.int32)[:, None] == (source + 72 * half)[None, :]
        return jnp.dot(stacked, chosen.astype(BF), preferred_element_type=F32).astype(BF)

    keep, give = pick(xl), pick(1 - xl)
    own = rows_from_slices(jnp.stack([p_img, p_txt]), xh, c)
    r = lax.rsqrt(jnp.sum(own * own, axis=2, keepdims=True) + 1e-06)
    z = (own * r).astype(BF)
    z, keep, give = lax.optimization_barrier((z, keep, give))
    z_img, z_txt = z[0], z[1]
    r_img, r_txt = r[0], r[1]

    img = jnp.broadcast_to(z_img[None], (16, 40, 1152))
    img, z_near = lax.optimization_barrier((img, z_txt))
    img = a2a(img, PLANE).reshape(640, 1152)
    up, down = [z_near], [z_near]
    for d in range(3):
        up.append(shift(up[-1], "z", 8, 1))
        down.append(shift(down[-1], "z", 8, -1))
    up.append(shift(up[-1], "z", 8, 1))
    txt_own = up + down[:0:-1]
    txt_oth = [swap_core(piece) for piece in txt_own]
    give, img = lax.optimization_barrier((give, img))
    come = lax.ppermute(give, "xl", [(0, 1), (1, 0)])
    first, second = jnp.where(xl == 0, keep, come), jnp.where(xl == 0, come, keep)
    fi = jnp.concatenate([first[:160], second[:160]])
    ft = jnp.concatenate([first[160:], second[160:]])

    place = (xl * 4 + y) * 2 + xh
    scalars = jnp.concatenate([jnp.exp(log_scale), bias])
    t_oth, t_own, g_img = block_grads(scalars, place.astype(jnp.int32).reshape(1), img, txt_oth + txt_own)
    t_got = swap_core(t_oth)
    t_sum = t_own + t_got.astype(F32)
    t_out = t_sum[40:].astype(BF)
    gz_txt = t_sum[:40]
    for d in range(1, 8):
        gz_txt = gz_txt + shift(t_out[40 * d - 40 : 40 * d], "z", 8, -d).astype(F32)
    g_img = g_img.reshape(16, 40, 1152)
    gz_img = jnp.sum(a2a(g_img, PLANE).astype(F32), axis=0)

    gz = jnp.stack([gz_img, gz_txt])
    values = z.astype(F32)
    inner = jnp.sum(values * gz, axis=2, keepdims=True)
    gp_rows = (r * (gz - values * inner)).astype(BF)
    cut = gp_rows.reshape(2, 40, 4, 288).transpose(2, 0, 1, 3)
    rest = jnp.concatenate([cut[:, 0, :, 256:], cut[:, 1, :, 256:], jnp.zeros((4, 40, 64), BF)], axis=2)
    piece = jnp.concatenate(
        [cut[:, :, :, :128].reshape(4, 80, 128), cut[:, :, :, 128:256].reshape(4, 80, 128), rest], axis=1
    )
    got = a2a(jnp.broadcast_to(piece[None], (2, 4, 200, 128)).reshape(8, 200, 128), ("xl", "xh", "c"))
    a_img, a_txt, b_img, b_txt, rest = (got[:, 40 * i : 40 * i + 40].reshape(320, 128) for i in range(5))

    def rows_dot(x, g):
        return jnp.einsum("rd,re->de", x, g, preferred_element_type=F32)

    lane = jnp.arange(128, dtype=jnp.int32)[None, :]
    rest_img = jnp.where(lane < 32, rest, jnp.zeros_like(rest))
    rest_txt = jnp.where(lane < 32, jnp.zeros_like(rest), rest)
    w = jnp.concatenate(
        [
            rows_dot(fi, jnp.concatenate([a_img, b_img], axis=1)),
            rows_dot(ft, jnp.concatenate([a_txt, b_txt], axis=1)),
            rows_dot(fi, rest_img) + rows_dot(ft, rest_txt),
        ],
        axis=1,
    ).reshape(4, 144, 640)
    up = lax.dynamic_index_in_dim(w, (y + 2) % 4, 0, keepdims=False).astype(BF)
    down = lax.dynamic_index_in_dim(w, (y + 3) % 4, 0, keepdims=False).astype(BF)
    up = shift(up, "y", 4, 1).astype(F32) + lax.dynamic_index_in_dim(w, (y + 1) % 4, 0, keepdims=False)
    w = lax.dynamic_index_in_dim(w, y, 0, keepdims=False) + shift(down, "y", 4, -1).astype(F32)
    w = w + shift(up.astype(BF), "y", 4, 1).astype(F32)
    w = jnp.sum(a2a(w.astype(BF).reshape(8, 18, 640), ("z",)).astype(F32), axis=0)
    w_img = jnp.concatenate([w[:, :256], w[:, 512:544]], axis=1)
    w_txt = jnp.concatenate([w[:, 256:512], w[:, 544:576]], axis=1)

    mine = lax.dynamic_slice_in_dim(got, xl * 4, 4, 0)
    mine = [mine[:, 40 * i : 40 * i + 40].reshape(160, 128) for i in range(5)]
    gp_img = jnp.concatenate([mine[0], mine[2], mine[4][:, :32]], axis=1)
    gp_txt = jnp.concatenate([mine[1], mine[3], mine[4][:, 32:64]], axis=1)

    def feature_part(to):
        out = [
            jnp.einsum("re,de->rd", g, lax.dynamic_slice_in_dim(p, to * 288, 288, 0), preferred_element_type=F32)
            for g, p in ((gp_img, image_proj), (gp_txt, text_proj))
        ]
        return jnp.stack(out)

    f = feature_part(xh * 2 + c)
    for dx, dc in ((0, 1), (1, 0), (1, 1)):
        other = feature_part((xh ^ dx) * 2 + (c ^ dc)).astype(BF)
        f = f + mp_shift(other, dx, dc).astype(F32)
    return f[0], f[1], w_img, w_txt


def solution(mesh):
    fine = Mesh(mesh.devices.reshape(SIZES), AXES)
    in_specs = (P(DP, None), P(DP, None), P(None, MP), P(None, MP), P(), P())
    out_specs = (P(DP, MP), P(DP, MP), P(DP, MP), P(DP, MP))
    return jax.shard_map(shards, mesh=fine, in_specs=in_specs, out_specs=out_specs, check_vma=False)
```

```python
import jax
import jax.numpy as jnp
from jax import lax
from jax.experimental import pallas as pl
from jax.experimental.pallas import tpu as pltpu
from jax.sharding import Mesh, PartitionSpec as P

AXES = ("z", "xl", "y", "xh", "c")
SIZES = (8, 2, 4, 2, 2)
DP = ("z", "xl", "y")
MP = ("xh", "c")
PLANE = ("xl", "y", "xh")
BF = jnp.bfloat16
F32 = jnp.float32


def a2a(x, axes):
    return lax.all_to_all(x, axes, 0, 0, tiled=True)


def swap_core(x):
    return lax.ppermute(x, "c", [(0, 1), (1, 0)])


def shift(x, axis, size, step):
    return lax.ppermute(x, axis, [(i, (i + step) % size) for i in range(size)])


def mp_shift(x, dx, dc):
    pairs = [(a * 2 + b, (a ^ dx) * 2 + (b ^ dc)) for a in range(2) for b in range(2)]
    return lax.ppermute(x, MP, pairs)


def rows_from_slices(pair, xh, c):
    quarters = pair.reshape(2, 2, 2, 40, 288)
    got = {}
    for dx in range(2):
        for dc in range(2):
            to = lax.dynamic_index_in_dim(quarters, xh ^ dx, 1, keepdims=False)
            to = lax.dynamic_index_in_dim(to, c ^ dc, 1, keepdims=False)
            got[dx, dc] = mp_shift(to, dx, dc) if dx or dc else to
    parts = []
    for a in range(2):
        for b in range(2):
            near = jnp.where(c == b, got[0, 0], got[0, 1])
            far = jnp.where(c == b, got[1, 0], got[1, 1])
            parts.append(jnp.where(xh == a, near, far))
    return jnp.concatenate(parts, axis=2)


def block_kernel(scalars, place, img_in, *refs):
    pieces = refs[:16]
    to_oth, to_own, to_img, img, parts, texts, coef, coef_t, t_oth, t_own, g_img, sems, out_sems = refs[16:]
    copies = [pltpu.make_async_copy(pieces[d], parts.at[d], sems.at[d]) for d in range(16)]
    copies.append(pltpu.make_async_copy(img_in, img, sems.at[16]))
    for copy in copies:
        copy.start()
    for d in range(8):
        copies[2 * d].wait()
        copies[2 * d + 1].wait()
        texts[80 * d : 80 * d + 80, :] = jnp.concatenate([parts[2 * d], parts[2 * d + 1]])
    copies[16].wait()
    scale, offset = scalars[0], scalars[1]
    dots = lax.dot_general(img[...], texts[...], (((1,), (1,)), ((), ())), preferred_element_type=F32)
    rows = lax.broadcasted_iota(jnp.int32, (640, 640), 0) - place[0] * 40
    cols = lax.broadcasted_iota(jnp.int32, (640, 640), 1) - 320
    sign = jnp.where((rows == cols) & (cols >= 0) & (cols < 40), F32(1.0), F32(-1.0))
    value = (-sign * scale * jax.nn.sigmoid(-sign * (scale * dots + offset))).astype(BF)
    coef[...] = value
    coef_t[...] = value.T
    sends = [
        pltpu.make_async_copy(t_oth, to_oth, out_sems.at[0]),
        pltpu.make_async_copy(t_own, to_own, out_sems.at[1]),
        pltpu.make_async_copy(g_img.at[pl.ds(0, 320)], to_img.at[pl.ds(0, 320)], out_sems.at[2]),
        pltpu.make_async_copy(g_img.at[pl.ds(320, 320)], to_img.at[pl.ds(320, 320)], out_sems.at[3]),
    ]
    t_oth[...] = jnp.dot(coef_t[:320, :], img[...], preferred_element_type=F32).astype(BF)
    sends[0].start()
    t_own[...] = jnp.dot(coef_t[320:, :], img[...], preferred_element_type=F32)
    sends[1].start()
    for half in range(2):
        at = 320 * half
        g_img[at : at + 320, :] = jnp.dot(
            coef[at : at + 320, :], texts[...], preferred_element_type=F32
        ).astype(BF)
        sends[2 + half].start()
    for send in sends:
        send.wait()


def block_grads(scalars, place, img, pieces):
    small = pl.BlockSpec(memory_space=pltpu.SMEM)
    large = pl.BlockSpec(memory_space=pltpu.HBM)
    return pl.pallas_call(
        block_kernel,
        out_shape=[
            jax.ShapeDtypeStruct((320, 1152), BF),
            jax.ShapeDtypeStruct((320, 1152), F32),
            jax.ShapeDtypeStruct((640, 1152), BF),
        ],
        in_specs=[small, small] + [large] * 17,
        out_specs=[large] * 3,
        scratch_shapes=[
            pltpu.VMEM((640, 1152), BF),
            pltpu.VMEM((16, 40, 1152), BF),
            pltpu.VMEM((640, 1152), BF),
            pltpu.VMEM((640, 640), BF),
            pltpu.VMEM((640, 640), BF),
            pltpu.VMEM((320, 1152), BF),
            pltpu.VMEM((320, 1152), F32),
            pltpu.VMEM((640, 1152), BF),
            pltpu.SemaphoreType.DMA((17,)),
            pltpu.SemaphoreType.DMA((4,)),
        ],
        compiler_params=pltpu.CompilerParams(vmem_limit_bytes=60 * 2**20),
        cost_estimate=pl.CostEstimate(flops=2900000000, bytes_accessed=8000000, transcendentals=400000),
    )(scalars, place, img, *pieces)


def shards(image_features, text_features, image_proj, text_proj, log_scale, bias):
    xl, y, xh, c = (lax.axis_index(a) for a in AXES[1:])
    p_img = jnp.dot(image_features, image_proj, preferred_element_type=F32)
    p_txt = jnp.dot(text_features, text_proj, preferred_element_type=F32)
    stacked = jnp.concatenate(lax.optimization_barrier((image_features, text_features, p_img, p_txt))[:2])
    col = jnp.arange(576, dtype=jnp.int32)
    source = (col % 144) // 18 * 144 + col // 144 * 18 + col % 18

    def pick(half):
        chosen = jnp.arange(1152, dtype=jnp.int32)[:, None] == (source + 72 * half)[None, :]
        return jnp.dot(stacked, chosen.astype(BF), preferred_element_type=F32).astype(BF)

    keep, give = pick(xl), pick(1 - xl)
    own = rows_from_slices(jnp.stack([p_img, p_txt]), xh, c)
    r = lax.rsqrt(jnp.sum(own * own, axis=2, keepdims=True) + 1e-06)
    z = (own * r).astype(BF)
    z, keep, give = lax.optimization_barrier((z, keep, give))
    z_img, z_txt = z[0], z[1]
    r_img, r_txt = r[0], r[1]

    img = jnp.broadcast_to(z_img[None], (16, 40, 1152))
    img, z_near = lax.optimization_barrier((img, z_txt))
    img = a2a(img, PLANE).reshape(640, 1152)
    come = lax.ppermute(give, "xl", [(0, 1), (1, 0)])
    up, down = [z_near], [z_near]
    for d in range(3):
        up.append(shift(up[-1], "z", 8, 1))
        down.append(shift(down[-1], "z", 8, -1))
        if d == 1:
            up[2], come = lax.optimization_barrier((up[2], come))
    up.append(shift(up[-1], "z", 8, 1))
    txt_own = up + down[:0:-1]
    txt_oth = [swap_core(piece) for piece in txt_own]
    first, second = jnp.where(xl == 0, keep, come), jnp.where(xl == 0, come, keep)
    fi = jnp.concatenate([first[:160], second[:160]])
    ft = jnp.concatenate([first[160:], second[160:]])

    place = (xl * 4 + y) * 2 + xh
    scalars = jnp.concatenate([jnp.exp(log_scale), bias])
    t_oth, t_own, g_img = block_grads(scalars, place.astype(jnp.int32).reshape(1), img, txt_oth + txt_own)
    t_got = swap_core(t_oth)
    t_sum = t_own + t_got.astype(F32)
    t_out = t_sum[40:].astype(BF)
    gz_txt = t_sum[:40]
    for d in range(1, 8):
        gz_txt = gz_txt + shift(t_out[40 * d - 40 : 40 * d], "z", 8, -d).astype(F32)
    g_img = g_img.reshape(16, 40, 1152)
    gz_img = jnp.sum(a2a(g_img, PLANE).astype(F32), axis=0)

    gz = jnp.stack([gz_img, gz_txt])
    values = z.astype(F32)
    inner = jnp.sum(values * gz, axis=2, keepdims=True)
    gp_rows = (r * (gz - values * inner)).astype(BF)
    cut = gp_rows.reshape(2, 40, 4, 288).transpose(2, 0, 1, 3)
    rest = jnp.concatenate([cut[:, 0, :, 256:], cut[:, 1, :, 256:], jnp.zeros((4, 40, 64), BF)], axis=2)
    piece = jnp.concatenate(
        [cut[:, :, :, :128].reshape(4, 80, 128), cut[:, :, :, 128:256].reshape(4, 80, 128), rest], axis=1
    )
    got = a2a(jnp.broadcast_to(piece[None], (2, 4, 200, 128)).reshape(8, 200, 128), ("xl", "xh", "c"))
    a_img, a_txt, b_img, b_txt, rest = (got[:, 40 * i : 40 * i + 40].reshape(320, 128) for i in range(5))

    def rows_dot(x, g):
        return jnp.einsum("rd,re->de", x, g, preferred_element_type=F32)

    lane = jnp.arange(128, dtype=jnp.int32)[None, :]
    rest_img = jnp.where(lane < 32, rest, jnp.zeros_like(rest))
    rest_txt = jnp.where(lane < 32, jnp.zeros_like(rest), rest)
    w = jnp.concatenate(
        [
            rows_dot(fi, jnp.concatenate([a_img, b_img], axis=1)),
            rows_dot(ft, jnp.concatenate([a_txt, b_txt], axis=1)),
            rows_dot(fi, rest_img) + rows_dot(ft, rest_txt),
        ],
        axis=1,
    ).reshape(4, 144, 640)
    up = lax.dynamic_index_in_dim(w, (y + 2) % 4, 0, keepdims=False).astype(BF)
    down = lax.dynamic_index_in_dim(w, (y + 3) % 4, 0, keepdims=False).astype(BF)
    up = shift(up, "y", 4, 1).astype(F32) + lax.dynamic_index_in_dim(w, (y + 1) % 4, 0, keepdims=False)
    w = lax.dynamic_index_in_dim(w, y, 0, keepdims=False) + shift(down, "y", 4, -1).astype(F32)
    w = w + shift(up.astype(BF), "y", 4, 1).astype(F32)
    w = jnp.sum(a2a(w.astype(BF).reshape(8, 18, 640), ("z",)).astype(F32), axis=0)
    w_img = jnp.concatenate([w[:, :256], w[:, 512:544]], axis=1)
    w_txt = jnp.concatenate([w[:, 256:512], w[:, 544:576]], axis=1)

    mine = lax.dynamic_slice_in_dim(got, xl * 4, 4, 0)
    mine = [mine[:, 40 * i : 40 * i + 40].reshape(160, 128) for i in range(5)]
    gp_img = jnp.concatenate([mine[0], mine[2], mine[4][:, :32]], axis=1)
    gp_txt = jnp.concatenate([mine[1], mine[3], mine[4][:, 32:64]], axis=1)

    def feature_part(to):
        out = [
            jnp.einsum("re,de->rd", g, lax.dynamic_slice_in_dim(p, to * 288, 288, 0), preferred_element_type=F32)
            for g, p in ((gp_img, image_proj), (gp_txt, text_proj))
        ]
        return jnp.stack(out)

    f = feature_part(xh * 2 + c)
    for dx, dc in ((0, 1), (1, 0), (1, 1)):
        other = feature_part((xh ^ dx) * 2 + (c ^ dc)).astype(BF)
        f = f + mp_shift(other, dx, dc).astype(F32)
    return f[0], f[1], w_img, w_txt


def solution(mesh):
    fine = Mesh(mesh.devices.reshape(SIZES), AXES)
    in_specs = (P(DP, None), P(DP, None), P(None, MP), P(None, MP), P(), P())
    out_specs = (P(DP, MP), P(DP, MP), P(DP, MP), P(DP, MP))
    return jax.shard_map(shards, mesh=fine, in_specs=in_specs, out_specs=out_specs, check_vma=False)
```

```python
import jax
import jax.numpy as jnp
from jax import lax
from jax.experimental import pallas as pl
from jax.experimental.pallas import tpu as pltpu
from jax.sharding import Mesh, PartitionSpec as P

AXES = ("z", "xl", "y", "xh", "c")
SIZES = (8, 2, 4, 2, 2)
DP = ("z", "xl", "y")
MP = ("xh", "c")
PLANE = ("xl", "y", "xh")
BF = jnp.bfloat16
F32 = jnp.float32


def a2a(x, axes):
    return lax.all_to_all(x, axes, 0, 0, tiled=True)


def swap_core(x):
    return lax.ppermute(x, "c", [(0, 1), (1, 0)])


def shift(x, axis, size, step):
    return lax.ppermute(x, axis, [(i, (i + step) % size) for i in range(size)])


def mp_shift(x, dx, dc):
    pairs = [(a * 2 + b, (a ^ dx) * 2 + (b ^ dc)) for a in range(2) for b in range(2)]
    return lax.ppermute(x, MP, pairs)


def rows_from_slices(pair, xh, c):
    quarters = pair.reshape(2, 2, 2, 40, 288)
    got = {}
    for dx in range(2):
        for dc in range(2):
            to = lax.dynamic_index_in_dim(quarters, xh ^ dx, 1, keepdims=False)
            to = lax.dynamic_index_in_dim(to, c ^ dc, 1, keepdims=False)
            got[dx, dc] = mp_shift(to, dx, dc) if dx or dc else to
    parts = []
    for a in range(2):
        for b in range(2):
            near = jnp.where(c == b, got[0, 0], got[0, 1])
            far = jnp.where(c == b, got[1, 0], got[1, 1])
            parts.append(jnp.where(xh == a, near, far))
    return jnp.concatenate(parts, axis=2)


def block_kernel(scalars, place, img_in, *refs):
    pieces = refs[:16]
    to_oth, to_own, to_img, img, parts, texts, coef, coef_t, t_oth, t_own, g_img, sems, out_sems = refs[16:]
    copies = [pltpu.make_async_copy(pieces[d], parts.at[d], sems.at[d]) for d in range(16)]
    copies.append(pltpu.make_async_copy(img_in, img, sems.at[16]))
    for copy in copies:
        copy.start()
    for d in range(8):
        copies[2 * d].wait()
        copies[2 * d + 1].wait()
        texts[80 * d : 80 * d + 80, :] = jnp.concatenate([parts[2 * d], parts[2 * d + 1]])
    copies[16].wait()
    scale, offset = scalars[0], scalars[1]
    dots = lax.dot_general(img[...], texts[...], (((1,), (1,)), ((), ())), preferred_element_type=F32)
    rows = lax.broadcasted_iota(jnp.int32, (640, 640), 0) - place[0] * 40
    cols = lax.broadcasted_iota(jnp.int32, (640, 640), 1) - 320
    sign = jnp.where((rows == cols) & (cols >= 0) & (cols < 40), F32(1.0), F32(-1.0))
    value = (-sign * scale * jax.nn.sigmoid(-sign * (scale * dots + offset))).astype(BF)
    coef[...] = value
    coef_t[...] = value.T
    sends = [
        pltpu.make_async_copy(t_oth, to_oth, out_sems.at[0]),
        pltpu.make_async_copy(t_own, to_own, out_sems.at[1]),
        pltpu.make_async_copy(g_img.at[pl.ds(0, 320)], to_img.at[pl.ds(0, 320)], out_sems.at[2]),
        pltpu.make_async_copy(g_img.at[pl.ds(320, 320)], to_img.at[pl.ds(320, 320)], out_sems.at[3]),
    ]
    t_oth[...] = jnp.dot(coef_t[:320, :], img[...], preferred_element_type=F32).astype(BF)
    sends[0].start()
    t_own[...] = jnp.dot(coef_t[320:, :], img[...], preferred_element_type=F32)
    sends[1].start()
    for half in range(2):
        at = 320 * half
        g_img[at : at + 320, :] = jnp.dot(
            coef[at : at + 320, :], texts[...], preferred_element_type=F32
        ).astype(BF)
        sends[2 + half].start()
    for send in sends:
        send.wait()


def block_grads(scalars, place, img, pieces):
    small = pl.BlockSpec(memory_space=pltpu.SMEM)
    large = pl.BlockSpec(memory_space=pltpu.HBM)
    return pl.pallas_call(
        block_kernel,
        out_shape=[
            jax.ShapeDtypeStruct((320, 1152), BF),
            jax.ShapeDtypeStruct((320, 1152), F32),
            jax.ShapeDtypeStruct((640, 1152), BF),
        ],
        in_specs=[small, small] + [large] * 17,
        out_specs=[large] * 3,
        scratch_shapes=[
            pltpu.VMEM((640, 1152), BF),
            pltpu.VMEM((16, 40, 1152), BF),
            pltpu.VMEM((640, 1152), BF),
            pltpu.VMEM((640, 640), BF),
            pltpu.VMEM((640, 640), BF),
            pltpu.VMEM((320, 1152), BF),
            pltpu.VMEM((320, 1152), F32),
            pltpu.VMEM((640, 1152), BF),
            pltpu.SemaphoreType.DMA((17,)),
            pltpu.SemaphoreType.DMA((4,)),
        ],
        compiler_params=pltpu.CompilerParams(vmem_limit_bytes=60 * 2**20),
        cost_estimate=pl.CostEstimate(flops=2900000000, bytes_accessed=8000000, transcendentals=400000),
    )(scalars, place, img, *pieces)


def shards(image_features, text_features, image_proj, text_proj, log_scale, bias):
    xl, y, xh, c = (lax.axis_index(a) for a in AXES[1:])
    p_img = jnp.dot(image_features, image_proj, preferred_element_type=F32)
    p_txt = jnp.dot(text_features, text_proj, preferred_element_type=F32)
    stacked = jnp.concatenate(lax.optimization_barrier((image_features, text_features, p_img, p_txt))[:2])
    col = jnp.arange(576, dtype=jnp.int32)
    source = (col % 144) // 18 * 144 + col // 144 * 18 + col % 18

    def pick(half, rows):
        chosen = jnp.arange(1152, dtype=jnp.int32)[:, None] == (source + 72 * half)[None, :]
        return jnp.dot(rows, chosen.astype(BF), preferred_element_type=F32).astype(BF)

    keep = pick(xl, stacked)
    give = pick(1 - xl, lax.dynamic_slice_in_dim(stacked, c * 160, 160, 0))
    own = rows_from_slices(jnp.stack([p_img, p_txt]), xh, c)
    r = lax.rsqrt(jnp.sum(own * own, axis=2, keepdims=True) + 1e-06)
    z = (own * r).astype(BF)
    z, keep, give = lax.optimization_barrier((z, keep, give))
    z_img, z_txt = z[0], z[1]
    r_img, r_txt = r[0], r[1]

    img = jnp.broadcast_to(z_img[None], (16, 40, 1152))
    img, z_near = lax.optimization_barrier((img, z_txt))
    img = a2a(img, PLANE).reshape(640, 1152)
    up, down = [z_near], [z_near]
    for d in range(3):
        up.append(shift(up[-1], "z", 8, 1))
        down.append(shift(down[-1], "z", 8, -1))
    up.append(shift(up[-1], "z", 8, 1))
    txt_own = up + down[:0:-1]
    txt_oth = [swap_core(piece) for piece in txt_own]
    give, img = lax.optimization_barrier((give, img))
    come = lax.ppermute(give, "xl", [(0, 1), (1, 0)])
    place = (xl * 4 + y) * 2 + xh
    scalars = jnp.concatenate([jnp.exp(log_scale), bias])
    t_oth, t_own, g_img = block_grads(scalars, place.astype(jnp.int32).reshape(1), img, txt_oth + txt_own)
    t_oth, come = lax.optimization_barrier((t_oth, come))
    t_got = swap_core(t_oth)
    come_oth = swap_core(come)
    come = jnp.concatenate([jnp.where(c == 0, come, come_oth), jnp.where(c == 0, come_oth, come)])
    first, second = jnp.where(xl == 0, keep, come), jnp.where(xl == 0, come, keep)
    fi = jnp.concatenate([first[:160], second[:160]])
    ft = jnp.concatenate([first[160:], second[160:]])

    t_sum = t_own + t_got.astype(F32)
    to = {k: t_sum[40 * (-k % 8) : 40 * (-k % 8) + 40] for k in range(-3, 5)}
    far_up = shift(jnp.concatenate([to[4], to[3]]).astype(BF), "z", 8, 2).astype(F32)
    far_down = shift(jnp.concatenate([to[-3], to[-2]]).astype(BF), "z", 8, -2).astype(F32)
    near = [
        shift((to[2] + far_up[:40]).astype(BF), "z", 8, 2),
        shift((to[1] + far_up[40:]).astype(BF), "z", 8, 1),
        shift((to[-1] + far_down[:40]).astype(BF), "z", 8, -1),
    ]
    gz_txt = to[0] + far_down[40:] + near[0].astype(F32) + near[1].astype(F32) + near[2].astype(F32)
    g_img = g_img.reshape(16, 40, 1152)
    gz_img = jnp.sum(a2a(g_img, PLANE).astype(F32), axis=0)

    gz = jnp.stack([gz_img, gz_txt])
    values = z.astype(F32)
    inner = jnp.sum(values * gz, axis=2, keepdims=True)
    gp_rows = (r * (gz - values * inner)).astype(BF)
    cut = gp_rows.reshape(2, 40, 4, 288).transpose(2, 0, 1, 3)
    rest = jnp.concatenate([cut[:, 0, :, 256:], cut[:, 1, :, 256:], jnp.zeros((4, 40, 64), BF)], axis=2)
    piece = jnp.concatenate(
        [cut[:, :, :, :128].reshape(4, 80, 128), cut[:, :, :, 128:256].reshape(4, 80, 128), rest], axis=1
    )
    got = a2a(jnp.broadcast_to(piece[None], (2, 4, 200, 128)).reshape(8, 200, 128), ("xl", "xh", "c"))
    a_img, a_txt, b_img, b_txt, rest = (got[:, 40 * i : 40 * i + 40].reshape(320, 128) for i in range(5))

    def rows_dot(x, g):
        return jnp.einsum("rd,re->de", x, g, preferred_element_type=F32)

    lane = jnp.arange(128, dtype=jnp.int32)[None, :]
    rest_img = jnp.where(lane < 32, rest, jnp.zeros_like(rest))
    rest_txt = jnp.where(lane < 32, jnp.zeros_like(rest), rest)
    w = jnp.concatenate(
        [
            rows_dot(fi, jnp.concatenate([a_img, b_img], axis=1)),
            rows_dot(ft, jnp.concatenate([a_txt, b_txt], axis=1)),
            rows_dot(fi, rest_img) + rows_dot(ft, rest_txt),
        ],
        axis=1,
    ).reshape(4, 144, 640)
    def block(k):
        return lax.dynamic_index_in_dim(w, (y + k) % 4, 0, keepdims=False)

    up, down = shift(block(2).astype(BF), "y", 4, 1), shift(block(3).astype(BF), "y", 4, -1)
    up = shift((up.astype(F32) + block(1)).astype(BF), "y", 4, 1)
    w = block(0) + down.astype(F32) + up.astype(F32)
    w = jnp.sum(a2a(w.astype(BF).reshape(8, 18, 640), ("z",)).astype(F32), axis=0)
    w_img = jnp.concatenate([w[:, :256], w[:, 512:544]], axis=1)
    w_txt = jnp.concatenate([w[:, 256:512], w[:, 544:576]], axis=1)

    mine = lax.dynamic_slice_in_dim(got, xl * 4, 4, 0)
    mine = [mine[:, 40 * i : 40 * i + 40].reshape(160, 128) for i in range(5)]
    gp_img = jnp.concatenate([mine[0], mine[2], mine[4][:, :32]], axis=1)
    gp_txt = jnp.concatenate([mine[1], mine[3], mine[4][:, 32:64]], axis=1)

    def feature_part(to):
        out = [
            jnp.einsum("re,de->rd", g, lax.dynamic_slice_in_dim(p, to * 288, 288, 0), preferred_element_type=F32)
            for g, p in ((gp_img, image_proj), (gp_txt, text_proj))
        ]
        return jnp.stack(out)

    f = feature_part(xh * 2 + c)
    for dx, dc in ((0, 1), (1, 0), (1, 1)):
        other = feature_part((xh ^ dx) * 2 + (c ^ dc)).astype(BF)
        f = f + mp_shift(other, dx, dc).astype(F32)
    return f[0], f[1], w_img, w_txt


def solution(mesh):
    fine = Mesh(mesh.devices.reshape(SIZES), AXES)
    in_specs = (P(DP, None), P(DP, None), P(None, MP), P(None, MP), P(), P())
    out_specs = (P(DP, MP), P(DP, MP), P(DP, MP), P(DP, MP))
    return jax.shard_map(shards, mesh=fine, in_specs=in_specs, out_specs=out_specs, check_vma=False)
```

```python
import jax
import jax.numpy as jnp
from jax import lax
from jax.experimental import pallas as pl
from jax.experimental.pallas import tpu as pltpu
from jax.sharding import Mesh, PartitionSpec as P

AXES = ("z", "xl", "y", "xh", "c")
SIZES = (8, 2, 4, 2, 2)
DP = ("z", "xl", "y")
MP = ("xh", "c")
PLANE = ("xl", "y", "xh")
BF = jnp.bfloat16
F32 = jnp.float32


def a2a(x, axes):
    return lax.all_to_all(x, axes, 0, 0, tiled=True)


def swap_core(x):
    return lax.ppermute(x, "c", [(0, 1), (1, 0)])


def shift(x, axis, size, step):
    return lax.ppermute(x, axis, [(i, (i + step) % size) for i in range(size)])


def apart(x):
    pairs = [(2 * i + k, (i + 1 - 2 * k) % 8 * 2 + k) for i in range(8) for k in range(2)]
    return lax.ppermute(x, ("z", "c"), pairs)


def mp_shift(x, dx, dc):
    pairs = [(a * 2 + b, (a ^ dx) * 2 + (b ^ dc)) for a in range(2) for b in range(2)]
    return lax.ppermute(x, MP, pairs)


def mp_exchange(part, xh, c):
    quarters = part.reshape(2, 2, 40, 288)
    got = {}
    for dx, dc in ((0, 0), (0, 1), (1, 0), (1, 1)):
        to = lax.dynamic_index_in_dim(quarters, xh ^ dx, 0, keepdims=False)
        to = lax.dynamic_index_in_dim(to, c ^ dc, 0, keepdims=False)
        got[dx, dc] = mp_shift(to, dx, dc) if dx or dc else to
    return got


def embed(got, xh, c):
    parts = []
    for a in range(2):
        for b in range(2):
            near = jnp.where(c == b, got[0, 0], got[0, 1])
            far = jnp.where(c == b, got[1, 0], got[1, 1])
            parts.append(jnp.where(xh == a, near, far))
    rows = jnp.concatenate(parts, axis=1)
    r = lax.rsqrt(jnp.sum(rows * rows, axis=1, keepdims=True) + 1e-06)
    return (rows * r).astype(BF), r


def block_kernel(scalars, place, img_in, *refs):
    pieces = refs[:11]
    to_oth, to_own, to_img, img, parts, texts, coef, coef_t, t_oth, t_own, g_img, sems, out_sems = refs[11:]
    core = place[1]
    far = 1 - core
    slots = [parts.at[0, core], parts.at[0, far]]
    slots += [parts.at[k + core * (8 - 2 * k)] for k in (1, 2, 3)] + [parts.at[4, core]]
    slots += [parts.at[k + far * (8 - 2 * k)] for k in (1, 2)]
    slots += [parts.at[3 + far * 2, 0], parts.at[3 + far * 2, 1], parts.at[4, far]]
    copies = [pltpu.make_async_copy(pieces[d], slots[d], sems.at[d]) for d in range(11)]
    copies.append(pltpu.make_async_copy(img_in, img, sems.at[11]))
    for copy in copies:
        copy.start()
    for copy in copies:
        copy.wait()
    for side in range(2):
        who = core if side else 1 - core
        for d in range(4):
            at = 320 * side + 80 * d
            texts[at : at + 80, :] = jnp.concatenate([parts[2 * d, who], parts[2 * d + 1, who]])
    scale, offset = scalars[0], scalars[1]
    dots = lax.dot_general(img[...], texts[...], (((1,), (1,)), ((), ())), preferred_element_type=F32)
    rows = lax.broadcasted_iota(jnp.int32, (640, 640), 0) - place[0] * 40
    cols = lax.broadcasted_iota(jnp.int32, (640, 640), 1) - 320
    sign = jnp.where((rows == cols) & (cols >= 0) & (cols < 40), F32(1.0), F32(-1.0))
    value = (-sign * scale * jax.nn.sigmoid(-sign * (scale * dots + offset))).astype(BF)
    coef[...] = value
    coef_t[...] = value.T
    sends = [
        pltpu.make_async_copy(t_oth, to_oth, out_sems.at[0]),
        pltpu.make_async_copy(t_own, to_own, out_sems.at[1]),
        pltpu.make_async_copy(g_img.at[pl.ds(0, 320)], to_img.at[pl.ds(0, 320)], out_sems.at[2]),
        pltpu.make_async_copy(g_img.at[pl.ds(320, 320)], to_img.at[pl.ds(320, 320)], out_sems.at[3]),
    ]
    t_oth[...] = jnp.dot(coef_t[:320, :], img[...], preferred_element_type=F32).astype(BF)
    sends[0].start()
    t_own[...] = jnp.dot(coef_t[320:, :], img[...], preferred_element_type=F32)
    sends[1].start()
    for half in range(2):
        at = 320 * half
        g_img[at : at + 320, :] = jnp.dot(
            coef[at : at + 320, :], texts[...], preferred_element_type=F32
        ).astype(BF)
        sends[2 + half].start()
    for send in sends:
        send.wait()


def block_grads(scalars, place, img, pieces):
    small = pl.BlockSpec(memory_space=pltpu.SMEM)
    large = pl.BlockSpec(memory_space=pltpu.HBM)
    return pl.pallas_call(
        block_kernel,
        out_shape=[
            jax.ShapeDtypeStruct((320, 1152), BF),
            jax.ShapeDtypeStruct((320, 1152), F32),
            jax.ShapeDtypeStruct((640, 1152), BF),
        ],
        in_specs=[small, small] + [large] * 12,
        out_specs=[large] * 3,
        scratch_shapes=[
            pltpu.VMEM((640, 1152), BF),
            pltpu.VMEM((8, 2, 40, 1152), BF),
            pltpu.VMEM((640, 1152), BF),
            pltpu.VMEM((640, 640), BF),
            pltpu.VMEM((640, 640), BF),
            pltpu.VMEM((320, 1152), BF),
            pltpu.VMEM((320, 1152), F32),
            pltpu.VMEM((640, 1152), BF),
            pltpu.SemaphoreType.DMA((12,)),
            pltpu.SemaphoreType.DMA((4,)),
        ],
        compiler_params=pltpu.CompilerParams(vmem_limit_bytes=60 * 2**20),
        cost_estimate=pl.CostEstimate(flops=2900000000, bytes_accessed=8000000, transcendentals=400000),
    )(scalars, place, img, *pieces)


def shards(image_features, text_features, image_proj, text_proj, log_scale, bias):
    xl, y, xh, c = (lax.axis_index(a) for a in AXES[1:])
    p_img = jnp.dot(image_features, image_proj, preferred_element_type=F32)
    p_txt = jnp.dot(text_features, text_proj, preferred_element_type=F32)
    stacked = jnp.concatenate(lax.optimization_barrier((image_features, text_features, p_img, p_txt))[:2])
    col = jnp.arange(576, dtype=jnp.int32)
    source = (col % 144) // 18 * 144 + col // 144 * 18 + col % 18

    def pick(half, rows):
        chosen = jnp.arange(1152, dtype=jnp.int32)[:, None] == (source + 72 * half)[None, :]
        return jnp.dot(rows, chosen.astype(BF), preferred_element_type=F32).astype(BF)

    keep = pick(xl, stacked)
    give = pick(1 - xl, lax.dynamic_slice_in_dim(stacked, c * 160, 160, 0))
    got_img = mp_exchange(p_img, xh, c)
    got_img[0, 1], p_txt = lax.optimization_barrier((got_img[0, 1], p_txt))
    got_txt = mp_exchange(p_txt, xh, c)
    z_img, r_img = embed(got_img, xh, c)
    z_txt, r_txt = embed(got_txt, xh, c)
    z_txt, keep, give = lax.optimization_barrier((z_txt, keep, give))

    img = jnp.broadcast_to(z_img[None], (16, 40, 1152))
    z_near = z_txt
    img = a2a(img, PLANE).reshape(640, 1152)
    z_far = swap_core(z_near)
    carried = [jnp.stack([jnp.where(c == 0, z_near, z_far), jnp.where(c == 0, z_far, z_near)])]
    for _ in range(3):
        carried.append(apart(carried[-1]))
    last, img = lax.optimization_barrier((carried[3], img))
    mine = carried[1:] + [shift(z_near, "z", 8, 4)]
    lower, upper = lax.optimization_barrier((swap_core(last[0]), last[1]))
    pieces = [z_near, z_far] + mine + [swap_core(mine[0]), swap_core(mine[1]), lower, swap_core(upper), swap_core(mine[3])]
    give, img = lax.optimization_barrier((give, img))
    come = lax.ppermute(give, "xl", [(0, 1), (1, 0)])
    place = jnp.stack([(xl * 4 + y) * 2 + xh, c]).astype(jnp.int32)
    scalars = jnp.concatenate([jnp.exp(log_scale), bias])
    t_oth, t_own, g_img = block_grads(scalars, place, img, pieces)
    t_oth, come = lax.optimization_barrier((t_oth, come))
    t_got = swap_core(t_oth)
    come_oth = swap_core(come)
    come = jnp.concatenate([jnp.where(c == 0, come, come_oth), jnp.where(c == 0, come_oth, come)])
    first, second = jnp.where(xl == 0, keep, come), jnp.where(xl == 0, come, keep)
    fi = jnp.concatenate([first[:160], second[:160]])
    ft = jnp.concatenate([first[160:], second[160:]])

    t_sum = t_own + t_got.astype(F32)
    to = {k: t_sum[40 * (-k % 8) : 40 * (-k % 8) + 40] for k in range(-3, 5)}
    far_up = shift(jnp.concatenate([to[4], to[3]]).astype(BF), "z", 8, 2).astype(F32)
    far_down = shift(jnp.concatenate([to[-3], to[-2]]).astype(BF), "z", 8, -2).astype(F32)
    far_up, z_img, z_txt, r_img, r_txt = lax.optimization_barrier((far_up, z_img, z_txt, r_img, r_txt))
    near = [
        shift((to[2] + far_up[:40]).astype(BF), "z", 8, 2),
        shift((to[1] + far_up[40:]).astype(BF), "z", 8, 1),
        shift((to[-1] + far_down[:40]).astype(BF), "z", 8, -1),
    ]
    gz_txt = to[0] + far_down[40:] + near[0].astype(F32) + near[1].astype(F32) + near[2].astype(F32)
    g_img = g_img.reshape(16, 40, 1152)
    gz_img = jnp.sum(a2a(g_img, PLANE).astype(F32), axis=0)

    gz = jnp.stack([gz_img, gz_txt])
    r = jnp.stack([r_img, r_txt])
    values = jnp.stack([z_img, z_txt]).astype(F32)
    inner = jnp.sum(values * gz, axis=2, keepdims=True)
    gp_rows = (r * (gz - values * inner)).astype(BF)
    cut = gp_rows.reshape(2, 40, 4, 288).transpose(2, 0, 1, 3)
    rest = jnp.concatenate([cut[:, 0, :, 256:], cut[:, 1, :, 256:]], axis=2)
    rest = jnp.concatenate([rest, rest], axis=2)
    piece = jnp.concatenate(
        [cut[:, :, :, :128].reshape(4, 80, 128), cut[:, :, :, 128:256].reshape(4, 80, 128), rest], axis=1
    )
    got = a2a(jnp.broadcast_to(piece[None], (2, 4, 200, 128)).reshape(8, 200, 128), ("xl", "xh", "c"))
    a_img, a_txt, b_img, b_txt, rest = (got[:, 40 * i : 40 * i + 40].reshape(320, 128) for i in range(5))

    def rows_dot(x, g):
        return jnp.einsum("rd,re->de", x, g, preferred_element_type=F32)

    lane = jnp.arange(128, dtype=jnp.int32)[None, :]
    w = jnp.concatenate(
        [
            rows_dot(fi, jnp.concatenate([a_img, b_img], axis=1)),
            rows_dot(ft, jnp.concatenate([a_txt, b_txt], axis=1)),
            jnp.where(lane < 32, rows_dot(fi, rest), rows_dot(ft, rest)),
        ],
        axis=1,
    ).reshape(4, 144, 640)
    def block(k):
        return lax.dynamic_index_in_dim(w, (y + k) % 4, 0, keepdims=False)

    up, down = shift(block(2).astype(BF), "y", 4, 1), shift(block(3).astype(BF), "y", 4, -1)
    up = shift((up.astype(F32) + block(1)).astype(BF), "y", 4, 1)
    w = block(0) + down.astype(F32) + up.astype(F32)
    w = jnp.sum(a2a(w.astype(BF).reshape(8, 18, 640), ("z",)).astype(F32), axis=0)
    w_img = jnp.concatenate([w[:, :256], w[:, 512:544]], axis=1)
    w_txt = jnp.concatenate([w[:, 256:512], w[:, 544:576]], axis=1)

    mine = lax.dynamic_slice_in_dim(got, xl * 4, 4, 0)
    mine = [mine[:, 40 * i : 40 * i + 40].reshape(160, 128) for i in range(5)]
    gp_img = jnp.concatenate([mine[0], mine[2], mine[4][:, :32]], axis=1)
    gp_txt = jnp.concatenate([mine[1], mine[3], mine[4][:, 32:64]], axis=1)

    def feature_part(to):
        out = [
            jnp.einsum("re,de->rd", g, lax.dynamic_slice_in_dim(p, to * 288, 288, 0), preferred_element_type=F32)
            for g, p in ((gp_img, image_proj), (gp_txt, text_proj))
        ]
        return jnp.stack(out)

    f = feature_part(xh * 2 + c)
    for dx, dc in ((0, 1), (1, 0), (1, 1)):
        other = feature_part((xh ^ dx) * 2 + (c ^ dc)).astype(BF)
        f = f + mp_shift(other, dx, dc).astype(F32)
    return f[0], f[1], w_img, w_txt


def solution(mesh):
    fine = Mesh(mesh.devices.reshape(SIZES), AXES)
    in_specs = (P(DP, None), P(DP, None), P(None, MP), P(None, MP), P(), P())
    out_specs = (P(DP, MP), P(DP, MP), P(DP, MP), P(DP, MP))
    return jax.shard_map(shards, mesh=fine, in_specs=in_specs, out_specs=out_specs, check_vma=False)
```

```python
import jax
import jax.numpy as jnp
from jax import lax
from jax.experimental import pallas as pl
from jax.experimental.pallas import tpu as pltpu
from jax.sharding import Mesh, PartitionSpec as P

AXES = ("z", "xl", "y", "xh", "c")
SIZES = (8, 2, 4, 2, 2)
DP = ("z", "xl", "y")
MP = ("xh", "c")
PLANE = ("xl", "y", "xh")
BF = jnp.bfloat16
F32 = jnp.float32


def a2a(x, axes):
    return lax.all_to_all(x, axes, 0, 0, tiled=True)


def swap_core(x):
    return lax.ppermute(x, "c", [(0, 1), (1, 0)])


def shift(x, axis, size, step):
    return lax.ppermute(x, axis, [(i, (i + step) % size) for i in range(size)])


def ring_sum(to):
    rows = to[0].shape[0]
    far_up = shift(jnp.concatenate([to[4], to[3]]).astype(BF), "z", 8, 2).astype(F32)
    far_down = shift(jnp.concatenate([to[-3], to[-2]]).astype(BF), "z", 8, -2).astype(F32)
    near = [
        shift((to[2] + far_up[:rows]).astype(BF), "z", 8, 2),
        shift((to[1] + far_up[rows:]).astype(BF), "z", 8, 1),
        shift((to[-1] + far_down[:rows]).astype(BF), "z", 8, -1),
    ]
    return to[0] + far_down[rows:] + near[0].astype(F32) + near[1].astype(F32) + near[2].astype(F32)


def mp_shift(x, dx, dc):
    pairs = [(a * 2 + b, (a ^ dx) * 2 + (b ^ dc)) for a in range(2) for b in range(2)]
    return lax.ppermute(x, MP, pairs)


def rows_from_slices(pair, xh, c):
    quarters = pair.reshape(2, 2, 2, 40, 288)
    got = {}
    for dx in range(2):
        for dc in range(2):
            to = lax.dynamic_index_in_dim(quarters, xh ^ dx, 1, keepdims=False)
            to = lax.dynamic_index_in_dim(to, c ^ dc, 1, keepdims=False)
            got[dx, dc] = mp_shift(to, dx, dc) if dx or dc else to
    parts = []
    for a in range(2):
        for b in range(2):
            near = jnp.where(c == b, got[0, 0], got[0, 1])
            far = jnp.where(c == b, got[1, 0], got[1, 1])
            parts.append(jnp.where(xh == a, near, far))
    return jnp.concatenate(parts, axis=2)


def block_kernel(scalars, place, img_in, *refs):
    pieces = refs[:16]
    to_oth, to_own, to_img, img, parts, texts, coef, coef_t, t_oth, t_own, g_img, sems, out_sems = refs[16:]
    copies = [pltpu.make_async_copy(pieces[d], parts.at[d], sems.at[d]) for d in range(16)]
    copies.append(pltpu.make_async_copy(img_in, img, sems.at[16]))
    for copy in copies:
        copy.start()
    for d in range(8):
        copies[2 * d].wait()
        copies[2 * d + 1].wait()
        texts[80 * d : 80 * d + 80, :] = jnp.concatenate([parts[2 * d], parts[2 * d + 1]])
    copies[16].wait()
    scale, offset = scalars[0], scalars[1]
    dots = lax.dot_general(img[...], texts[...], (((1,), (1,)), ((), ())), preferred_element_type=F32)
    rows = lax.broadcasted_iota(jnp.int32, (640, 640), 0) - place[0] * 40
    cols = lax.broadcasted_iota(jnp.int32, (640, 640), 1) - 320
    sign = jnp.where((rows == cols) & (cols >= 0) & (cols < 40), F32(1.0), F32(-1.0))
    value = (-sign * scale * jax.nn.sigmoid(-sign * (scale * dots + offset))).astype(BF)
    coef[...] = value
    coef_t[...] = value.T
    sends = [
        pltpu.make_async_copy(t_oth, to_oth, out_sems.at[0]),
        pltpu.make_async_copy(t_own, to_own, out_sems.at[1]),
        pltpu.make_async_copy(g_img.at[pl.ds(0, 320)], to_img.at[pl.ds(0, 320)], out_sems.at[2]),
        pltpu.make_async_copy(g_img.at[pl.ds(320, 320)], to_img.at[pl.ds(320, 320)], out_sems.at[3]),
    ]
    t_oth[...] = jnp.dot(coef_t[:320, :], img[...], preferred_element_type=F32).astype(BF)
    sends[0].start()
    t_own[...] = jnp.dot(coef_t[320:, :], img[...], preferred_element_type=F32)
    sends[1].start()
    for half in range(2):
        at = 320 * half
        g_img[at : at + 320, :] = jnp.dot(
            coef[at : at + 320, :], texts[...], preferred_element_type=F32
        ).astype(BF)
        sends[2 + half].start()
    for send in sends:
        send.wait()


def block_grads(scalars, place, img, pieces):
    small = pl.BlockSpec(memory_space=pltpu.SMEM)
    large = pl.BlockSpec(memory_space=pltpu.HBM)
    return pl.pallas_call(
        block_kernel,
        out_shape=[
            jax.ShapeDtypeStruct((320, 1152), BF),
            jax.ShapeDtypeStruct((320, 1152), F32),
            jax.ShapeDtypeStruct((640, 1152), BF),
        ],
        in_specs=[small, small] + [large] * 17,
        out_specs=[large] * 3,
        scratch_shapes=[
            pltpu.VMEM((640, 1152), BF),
            pltpu.VMEM((16, 40, 1152), BF),
            pltpu.VMEM((640, 1152), BF),
            pltpu.VMEM((640, 640), BF),
            pltpu.VMEM((640, 640), BF),
            pltpu.VMEM((320, 1152), BF),
            pltpu.VMEM((320, 1152), F32),
            pltpu.VMEM((640, 1152), BF),
            pltpu.SemaphoreType.DMA((17,)),
            pltpu.SemaphoreType.DMA((4,)),
        ],
        compiler_params=pltpu.CompilerParams(vmem_limit_bytes=60 * 2**20),
        cost_estimate=pl.CostEstimate(flops=2900000000, bytes_accessed=8000000, transcendentals=400000),
    )(scalars, place, img, *pieces)


def shards(image_features, text_features, image_proj, text_proj, log_scale, bias):
    zi, xl, y, xh, c = (lax.axis_index(a) for a in AXES)
    p_img = jnp.dot(image_features, image_proj, preferred_element_type=F32)
    p_txt = jnp.dot(text_features, text_proj, preferred_element_type=F32)
    stacked = jnp.concatenate(lax.optimization_barrier((image_features, text_features, p_img, p_txt))[:2])
    col = jnp.arange(576, dtype=jnp.int32)
    source = (col % 144 // 18 + zi) % 8 * 144 + col // 144 * 18 + col % 18

    def pick(half, rows):
        chosen = jnp.arange(1152, dtype=jnp.int32)[:, None] == (source + 72 * half)[None, :]
        return jnp.dot(rows, chosen.astype(BF), preferred_element_type=F32).astype(BF)

    keep = pick(xl, stacked)
    give = pick(1 - xl, lax.dynamic_slice_in_dim(stacked, c * 160, 160, 0))
    own = rows_from_slices(jnp.stack([p_img, p_txt]), xh, c)
    r = lax.rsqrt(jnp.sum(own * own, axis=2, keepdims=True) + 1e-06)
    z = (own * r).astype(BF)
    z, keep, give = lax.optimization_barrier((z, keep, give))
    z_img, z_txt = z[0], z[1]
    r_img, r_txt = r[0], r[1]

    img = jnp.broadcast_to(z_img[None], (16, 40, 1152))
    img, z_near = lax.optimization_barrier((img, z_txt))
    img = a2a(img, PLANE).reshape(640, 1152)
    four = shift(z_near, "z", 8, 4)
    up, down = [z_near], [z_near]
    for d in range(3):
        up.append(shift(up[-1], "z", 8, 1))
        down.append(shift(down[-1], "z", 8, -1))
    txt_own = up + [four] + down[:0:-1]
    last_up, last_down, img = lax.optimization_barrier((up[3], down[3], img))
    txt_oth = [swap_core(piece) for piece in up[:3] + [last_up, four, last_down] + down[2:0:-1]]
    give, img = lax.optimization_barrier((give, img))
    come = lax.ppermute(give, "xl", [(0, 1), (1, 0)])
    place = (xl * 4 + y) * 2 + xh
    scalars = jnp.concatenate([jnp.exp(log_scale), bias])
    t_oth, t_own, g_img = block_grads(scalars, place.astype(jnp.int32).reshape(1), img, txt_oth + txt_own)
    t_oth, come = lax.optimization_barrier((t_oth, come))
    t_got = swap_core(t_oth)
    come_oth = swap_core(come)
    come = jnp.concatenate([jnp.where(c == 0, come, come_oth), jnp.where(c == 0, come_oth, come)])
    first, second = jnp.where(xl == 0, keep, come), jnp.where(xl == 0, come, keep)
    fi = jnp.concatenate([first[:160], second[:160]])
    ft = jnp.concatenate([first[160:], second[160:]])

    t_sum = t_own + t_got.astype(F32)
    to = {k: t_sum[40 * (-k % 8) : 40 * (-k % 8) + 40] for k in range(-3, 5)}
    gz_txt = ring_sum(to)
    g_img = g_img.reshape(16, 40, 1152)
    gz_img = jnp.sum(a2a(g_img, PLANE).astype(F32), axis=0)

    gz = jnp.stack([gz_img, gz_txt])
    values = z.astype(F32)
    inner = jnp.sum(values * gz, axis=2, keepdims=True)
    gp_rows = (r * (gz - values * inner)).astype(BF)
    cut = gp_rows.reshape(2, 40, 4, 288).transpose(2, 0, 1, 3)
    rest = jnp.concatenate([cut[:, 0, :, 256:], cut[:, 1, :, 256:]], axis=2)
    rest = jnp.concatenate([rest, rest], axis=2)
    piece = jnp.concatenate(
        [cut[:, :, :, :128].reshape(4, 80, 128), cut[:, :, :, 128:256].reshape(4, 80, 128), rest], axis=1
    )
    got = a2a(jnp.broadcast_to(piece[None], (2, 4, 200, 128)).reshape(8, 200, 128), ("xl", "xh", "c"))
    a_img, a_txt, b_img, b_txt, rest = (got[:, 40 * i : 40 * i + 40].reshape(320, 128) for i in range(5))

    def rows_dot(x, g):
        return jnp.einsum("rd,re->de", x, g, preferred_element_type=F32)

    lane = lax.broadcasted_iota(jnp.int32, (576, 128), 1)
    w = jnp.concatenate(
        [
            rows_dot(fi, jnp.concatenate([a_img, b_img], axis=1)),
            rows_dot(ft, jnp.concatenate([a_txt, b_txt], axis=1)),
            jnp.where(lane < 32, rows_dot(fi, rest), rows_dot(ft, rest)),
        ],
        axis=1,
    ).reshape(4, 144, 640)
    def block(k):
        return lax.dynamic_index_in_dim(w, (y + k) % 4, 0, keepdims=False)

    up, down = shift(block(2).astype(BF), "y", 4, 1), shift(block(3).astype(BF), "y", 4, -1)
    up = shift((up.astype(F32) + block(1)).astype(BF), "y", 4, 1)
    w = block(0) + down.astype(F32) + up.astype(F32)
    w = ring_sum({k: w[18 * (k % 8) : 18 * (k % 8) + 18] for k in range(-3, 5)})
    w_img = jnp.concatenate([w[:, :256], w[:, 512:544]], axis=1)
    w_txt = jnp.concatenate([w[:, 256:512], w[:, 544:576]], axis=1)

    mine = lax.dynamic_slice_in_dim(got, xl * 4, 4, 0)
    mine = [mine[:, 40 * i : 40 * i + 40].reshape(160, 128) for i in range(5)]
    gp_img = jnp.concatenate([mine[0], mine[2], mine[4][:, :32]], axis=1)
    gp_txt = jnp.concatenate([mine[1], mine[3], mine[4][:, 32:64]], axis=1)

    def feature_part(to):
        out = [
            jnp.einsum("re,de->rd", g, lax.dynamic_slice_in_dim(p, to * 288, 288, 0), preferred_element_type=F32)
            for g, p in ((gp_img, image_proj), (gp_txt, text_proj))
        ]
        return jnp.stack(out)

    f = feature_part(xh * 2 + c)
    for dx, dc in ((0, 1), (1, 0), (1, 1)):
        other = feature_part((xh ^ dx) * 2 + (c ^ dc)).astype(BF)
        f = f + mp_shift(other, dx, dc).astype(F32)
    return f[0], f[1], w_img, w_txt


def solution(mesh):
    fine = Mesh(mesh.devices.reshape(SIZES), AXES)
    in_specs = (P(DP, None), P(DP, None), P(None, MP), P(None, MP), P(), P())
    out_specs = (P(DP, MP), P(DP, MP), P(DP, MP), P(DP, MP))
    return jax.shard_map(shards, mesh=fine, in_specs=in_specs, out_specs=out_specs, check_vma=False)
```

```python
import jax
import jax.numpy as jnp
from jax import lax
from jax.experimental import pallas as pl
from jax.experimental.pallas import tpu as pltpu
from jax.sharding import Mesh, PartitionSpec as P

AXES = ("z", "xl", "y", "xh", "c")
SIZES = (8, 2, 4, 2, 2)
DP = ("z", "xl", "y")
MP = ("xh", "c")
PLANE = ("xl", "y", "xh")
BF = jnp.bfloat16
F32 = jnp.float32


def a2a(x, axes):
    return lax.all_to_all(x, axes, 0, 0, tiled=True)


def swap_core(x):
    return lax.ppermute(x, "c", [(0, 1), (1, 0)])


def shift(x, axis, size, step):
    return lax.ppermute(x, axis, [(i, (i + step) % size) for i in range(size)])


def ring_sum(to):
    rows = to[0].shape[0]
    far_up = shift(jnp.concatenate([to[4], to[3]]).astype(BF), "z", 8, 2).astype(F32)
    far_down = shift(jnp.concatenate([to[-3], to[-2]]).astype(BF), "z", 8, -2).astype(F32)
    near = [
        shift((to[2] + far_up[:rows]).astype(BF), "z", 8, 2),
        shift((to[1] + far_up[rows:]).astype(BF), "z", 8, 1),
        shift((to[-1] + far_down[:rows]).astype(BF), "z", 8, -1),
    ]
    return to[0] + far_down[rows:] + near[0].astype(F32) + near[1].astype(F32) + near[2].astype(F32)


def mp_shift(x, dx, dc):
    pairs = [(a * 2 + b, (a ^ dx) * 2 + (b ^ dc)) for a in range(2) for b in range(2)]
    return lax.ppermute(x, MP, pairs)


def rows_from_slices(pair, xh, c):
    quarters = pair.reshape(2, 2, 2, 40, 288)
    got = {}
    for dx in range(2):
        for dc in range(2):
            to = lax.dynamic_index_in_dim(quarters, xh ^ dx, 1, keepdims=False)
            to = lax.dynamic_index_in_dim(to, c ^ dc, 1, keepdims=False)
            got[dx, dc] = mp_shift(to, dx, dc) if dx or dc else to
    parts = []
    for a in range(2):
        for b in range(2):
            near = jnp.where(c == b, got[0, 0], got[0, 1])
            far = jnp.where(c == b, got[1, 0], got[1, 1])
            parts.append(jnp.where(xh == a, near, far))
    return jnp.concatenate(parts, axis=2)


def block_kernel(scalars, place, img_in, *refs):
    pieces = refs[:16]
    to_oth, to_own, to_img, img, parts, texts, coef, coef_t, t_oth, t_own, g_img, sems, out_sems = refs[16:]
    copies = [pltpu.make_async_copy(pieces[d], parts.at[d], sems.at[d]) for d in range(16)]
    copies.append(pltpu.make_async_copy(img_in, img, sems.at[16]))
    for copy in copies:
        copy.start()
    for d in range(8):
        copies[2 * d].wait()
        copies[2 * d + 1].wait()
        texts[80 * d : 80 * d + 80, :] = jnp.concatenate([parts[2 * d], parts[2 * d + 1]])
    copies[16].wait()
    scale, offset = scalars[0], scalars[1]
    dots = lax.dot_general(img[...], texts[...], (((1,), (1,)), ((), ())), preferred_element_type=F32)
    rows = lax.broadcasted_iota(jnp.int32, (640, 640), 0) - place[0] * 40
    cols = lax.broadcasted_iota(jnp.int32, (640, 640), 1) - 320
    sign = jnp.where((rows == cols) & (cols >= 0) & (cols < 40), F32(1.0), F32(-1.0))
    value = (-sign * scale * jax.nn.sigmoid(-sign * (scale * dots + offset))).astype(BF)
    coef[...] = value
    coef_t[...] = value.T
    sends = [
        pltpu.make_async_copy(t_oth, to_oth, out_sems.at[0]),
        pltpu.make_async_copy(t_own, to_own, out_sems.at[1]),
        pltpu.make_async_copy(g_img.at[pl.ds(0, 320)], to_img.at[pl.ds(0, 320)], out_sems.at[2]),
        pltpu.make_async_copy(g_img.at[pl.ds(320, 320)], to_img.at[pl.ds(320, 320)], out_sems.at[3]),
    ]
    t_oth[...] = jnp.dot(coef_t[:320, :], img[...], preferred_element_type=F32).astype(BF)
    sends[0].start()
    t_own[...] = jnp.dot(coef_t[320:, :], img[...], preferred_element_type=F32).astype(BF)
    sends[1].start()
    for half in range(2):
        at = 320 * half
        g_img[at : at + 320, :] = jnp.dot(
            coef[at : at + 320, :], texts[...], preferred_element_type=F32
        ).astype(BF)
        sends[2 + half].start()
    for send in sends:
        send.wait()


def block_grads(scalars, place, img, pieces):
    small = pl.BlockSpec(memory_space=pltpu.SMEM)
    large = pl.BlockSpec(memory_space=pltpu.HBM)
    return pl.pallas_call(
        block_kernel,
        out_shape=[
            jax.ShapeDtypeStruct((320, 1152), BF),
            jax.ShapeDtypeStruct((320, 1152), BF),
            jax.ShapeDtypeStruct((640, 1152), BF),
        ],
        in_specs=[small, small] + [large] * 17,
        out_specs=[large] * 3,
        scratch_shapes=[
            pltpu.VMEM((640, 1152), BF),
            pltpu.VMEM((16, 40, 1152), BF),
            pltpu.VMEM((640, 1152), BF),
            pltpu.VMEM((640, 640), BF),
            pltpu.VMEM((640, 640), BF),
            pltpu.VMEM((320, 1152), BF),
            pltpu.VMEM((320, 1152), BF),
            pltpu.VMEM((640, 1152), BF),
            pltpu.SemaphoreType.DMA((17,)),
            pltpu.SemaphoreType.DMA((4,)),
        ],
        compiler_params=pltpu.CompilerParams(vmem_limit_bytes=60 * 2**20),
        cost_estimate=pl.CostEstimate(flops=2900000000, bytes_accessed=8000000, transcendentals=400000),
    )(scalars, place, img, *pieces)


def shards(image_features, text_features, image_proj, text_proj, log_scale, bias):
    xl, y, xh, c = (lax.axis_index(a) for a in AXES[1:])
    p_img = jnp.dot(image_features, image_proj, preferred_element_type=F32)
    p_txt = jnp.dot(text_features, text_proj, preferred_element_type=F32)
    stacked = jnp.concatenate(lax.optimization_barrier((image_features, text_features, p_img, p_txt))[:2])
    col = jnp.arange(576, dtype=jnp.int32)
    source = (col % 144) // 18 * 144 + col // 144 * 18 + col % 18

    def pick(half, rows):
        chosen = jnp.arange(1152, dtype=jnp.int32)[:, None] == (source + 72 * half)[None, :]
        return jnp.dot(rows, chosen.astype(BF), preferred_element_type=F32).astype(BF)

    keep = pick(xl, stacked)
    give = pick(1 - xl, lax.dynamic_slice_in_dim(stacked, c * 160, 160, 0))
    own = rows_from_slices(jnp.stack([p_img, p_txt]), xh, c)
    r = lax.rsqrt(jnp.sum(own * own, axis=2, keepdims=True) + 1e-06)
    z = (own * r).astype(BF)
    z, keep, give = lax.optimization_barrier((z, keep, give))
    z_img, z_txt = z[0], z[1]
    r_img, r_txt = r[0], r[1]

    img = jnp.broadcast_to(z_img[None], (16, 40, 1152))
    img, z_near = lax.optimization_barrier((img, z_txt))
    img = a2a(img, PLANE).reshape(640, 1152)
    four = shift(z_near, "z", 8, 4)
    up, down = [z_near], [z_near]
    for d in range(3):
        up.append(shift(up[-1], "z", 8, 1))
        down.append(shift(down[-1], "z", 8, -1))
    txt_own = up + [four] + down[:0:-1]
    last_up, last_down, img = lax.optimization_barrier((up[3], down[3], img))
    txt_oth = [swap_core(piece) for piece in up[:3] + [last_up, four, last_down] + down[2:0:-1]]
    give, img = lax.optimization_barrier((give, img))
    come = lax.ppermute(give, "xl", [(0, 1), (1, 0)])
    place = (xl * 4 + y) * 2 + xh
    scalars = jnp.concatenate([jnp.exp(log_scale), bias])
    t_oth, t_own, g_img = block_grads(scalars, place.astype(jnp.int32).reshape(1), img, txt_oth + txt_own)
    t_oth, come = lax.optimization_barrier((t_oth, come))
    t_got = swap_core(t_oth)
    come_oth = swap_core(come)
    come = jnp.concatenate([jnp.where(c == 0, come, come_oth), jnp.where(c == 0, come_oth, come)])
    first, second = jnp.where(xl == 0, keep, come), jnp.where(xl == 0, come, keep)
    fi = jnp.concatenate([first[:160], second[:160]])
    ft = jnp.concatenate([first[160:], second[160:]])

    t_sum = t_own.astype(F32) + t_got.astype(F32)
    to = {k: t_sum[40 * (-k % 8) : 40 * (-k % 8) + 40] for k in range(-3, 5)}
    gz_txt = ring_sum(to)
    g_img = g_img.reshape(16, 40, 1152)
    gz_img = jnp.sum(a2a(g_img, PLANE).astype(F32), axis=0)

    gz = jnp.stack([gz_img, gz_txt])
    values = z.astype(F32)
    inner = jnp.sum(values * gz, axis=2, keepdims=True)
    gp_rows = (r * (gz - values * inner)).astype(BF)
    cut = gp_rows.reshape(2, 40, 4, 288).transpose(2, 0, 1, 3)
    rest = jnp.concatenate([cut[:, 0, :, 256:], cut[:, 1, :, 256:]], axis=2)
    rest = jnp.concatenate([rest, rest], axis=2)
    piece = jnp.concatenate(
        [cut[:, :, :, :128].reshape(4, 80, 128), cut[:, :, :, 128:256].reshape(4, 80, 128), rest], axis=1
    )
    got = a2a(jnp.broadcast_to(piece[None], (2, 4, 200, 128)).reshape(8, 200, 128), ("xl", "xh", "c"))
    a_img, a_txt, b_img, b_txt, rest = (got[:, 40 * i : 40 * i + 40].reshape(320, 128) for i in range(5))

    def rows_dot(x, g):
        return jnp.einsum("rd,re->de", x, g, preferred_element_type=F32)

    lane, rest = lax.optimization_barrier((lax.broadcasted_iota(jnp.int32, (576, 128), 1), rest))
    w = jnp.concatenate(
        [
            rows_dot(fi, jnp.concatenate([a_img, b_img], axis=1)),
            rows_dot(ft, jnp.concatenate([a_txt, b_txt], axis=1)),
            jnp.where(lane < 32, rows_dot(fi, rest), rows_dot(ft, rest)),
        ],
        axis=1,
    ).reshape(4, 144, 640)
    def block(k):
        return lax.dynamic_index_in_dim(w, (y + k) % 4, 0, keepdims=False)

    up, down = shift(block(2).astype(BF), "y", 4, 1), shift(block(3).astype(BF), "y", 4, -1)
    up = shift((up.astype(F32) + block(1)).astype(BF), "y", 4, 1)
    w = block(0) + down.astype(F32) + up.astype(F32)
    w = jnp.sum(a2a(w.astype(BF).reshape(8, 18, 640), ("z",)).astype(F32), axis=0)
    w_img = jnp.concatenate([w[:, :256], w[:, 512:544]], axis=1)
    w_txt = jnp.concatenate([w[:, 256:512], w[:, 544:576]], axis=1)

    mine = lax.dynamic_slice_in_dim(got, xl * 4, 4, 0)
    mine = [mine[:, 40 * i : 40 * i + 40].reshape(160, 128) for i in range(5)]
    gp_img = jnp.concatenate([mine[0], mine[2], mine[4][:, :32]], axis=1)
    gp_txt = jnp.concatenate([mine[1], mine[3], mine[4][:, 32:64]], axis=1)

    def feature_part(to):
        out = [
            jnp.einsum("re,de->rd", g, lax.dynamic_slice_in_dim(p, to * 288, 288, 0), preferred_element_type=F32)
            for g, p in ((gp_img, image_proj), (gp_txt, text_proj))
        ]
        return jnp.stack(out)

    f = feature_part(xh * 2 + c)
    for dx, dc in ((0, 1), (1, 0), (1, 1)):
        other = feature_part((xh ^ dx) * 2 + (c ^ dc)).astype(BF)
        f = f + mp_shift(other, dx, dc).astype(F32)
    return f[0], f[1], w_img, w_txt


def solution(mesh):
    fine = Mesh(mesh.devices.reshape(SIZES), AXES)
    in_specs = (P(DP, None), P(DP, None), P(None, MP), P(None, MP), P(), P())
    out_specs = (P(DP, MP), P(DP, MP), P(DP, MP), P(DP, MP))
    return jax.shard_map(shards, mesh=fine, in_specs=in_specs, out_specs=out_specs, check_vma=False)
```

```python
import jax
import jax.numpy as jnp
from jax import lax
from jax.experimental import pallas as pl
from jax.experimental.pallas import tpu as pltpu
from jax.sharding import Mesh, PartitionSpec as P

AXES = ("z", "xl", "y", "xh", "c")
SIZES = (8, 2, 4, 2, 2)
DP = ("z", "xl", "y")
MP = ("xh", "c")
PLANE = ("xl", "y", "xh")
BF = jnp.bfloat16
F32 = jnp.float32


def a2a(x, axes):
    return lax.all_to_all(x, axes, 0, 0, tiled=True)


def swap_core(x):
    return lax.ppermute(x, "c", [(0, 1), (1, 0)])


def shift(x, axis, size, step):
    return lax.ppermute(x, axis, [(i, (i + step) % size) for i in range(size)])


def ring_sum(to):
    rows = to[0].shape[0]
    far_up = shift(jnp.concatenate([to[4], to[3]]).astype(BF), "z", 8, 2).astype(F32)
    far_down = shift(jnp.concatenate([to[-3], to[-2]]).astype(BF), "z", 8, -2).astype(F32)
    near = [
        shift((to[2] + far_up[:rows]).astype(BF), "z", 8, 2),
        shift((to[1] + far_up[rows:]).astype(BF), "z", 8, 1),
        shift((to[-1] + far_down[:rows]).astype(BF), "z", 8, -1),
    ]
    return to[0] + far_down[rows:] + near[0].astype(F32) + near[1].astype(F32) + near[2].astype(F32)


def mp_shift(x, dx, dc):
    pairs = [(a * 2 + b, (a ^ dx) * 2 + (b ^ dc)) for a in range(2) for b in range(2)]
    return lax.ppermute(x, MP, pairs)


def project_kernel(*refs):
    xh, c = lax.axis_index("xh"), lax.axis_index("c")
    ins, outs, held, flat, sems = refs[:4], refs[4:8], refs[8:12], refs[12], refs[13]
    copies = [pltpu.make_async_copy(ins[i], held[i], sems.at[i]) for i in range(4)]
    for copy in copies:
        copy.start()
    for i in range(2):
        copies[2 * i].wait()
        copies[2 * i + 1].wait()
        p = lax.dot_general(
            held[2 * i][...], held[2 * i + 1][...], (((1,), (1,)), ((), ())), preferred_element_type=F32
        )
        flat[i, :, :256] = p[:, :256]
        flat[i, :, 256:384] = jnp.concatenate([p[:, 256:], jnp.zeros((160, 96), F32)], axis=1)
    for d in range(4):
        at = pl.multiple_of(((xh ^ (d // 2)) * 2 + (c ^ (d % 2))) * 40, 8)
        for i in range(2):
            outs[d][80 * i : 80 * i + 40, :] = flat[i, pl.ds(at, 40), :128]
            outs[d][80 * i + 40 : 80 * i + 80, :] = flat[i, pl.ds(at, 40), 128:256]
        outs[d][160:200, :] = flat[0, pl.ds(at, 40), 256:384] + pltpu.roll(flat[1, pl.ds(at, 40), 256:384], 32, 1)


def project(image_features, image_proj, text_features, text_proj):
    return pl.pallas_call(
        project_kernel,
        out_shape=[jax.ShapeDtypeStruct((200, 128), F32)] * 4,
        in_specs=[pl.BlockSpec(memory_space=pltpu.HBM)] * 4,
        scratch_shapes=[pltpu.VMEM((160, 1152), BF), pltpu.VMEM((288, 1152), BF)] * 2
        + [pltpu.VMEM((2, 160, 384), F32), pltpu.SemaphoreType.DMA((4,))],
        compiler_params=pltpu.CompilerParams(vmem_limit_bytes=60 * 2**20),
        cost_estimate=pl.CostEstimate(flops=220000000, bytes_accessed=2500000, transcendentals=0),
    )(image_features, image_proj.T, text_features, text_proj.T)


def embed(pieces, xh, c):
    parts = []
    for a in range(2):
        for b in range(2):
            near = jnp.where(c == b, pieces[0], pieces[1])
            far = jnp.where(c == b, pieces[2], pieces[3])
            parts.append(jnp.where(xh == a, near, far))
    rows = []
    for i in range(2):
        cols = [part[80 * i + 40 * j : 80 * i + 40 * j + 40] for part in parts for j in range(2)]
        cols += [part[160:, 32 * i : 32 * i + 32] for part in parts]
        rows.append(jnp.concatenate(cols, axis=1))
    return jnp.stack(rows)


def block_kernel(scalars, place, img_in, *refs):
    pieces = refs[:16]
    to_oth, to_own, to_img, img, parts, texts, coef, coef_t, t_oth, t_own, g_img, sems, out_sems = refs[16:]
    copies = [pltpu.make_async_copy(pieces[d], parts.at[d], sems.at[d]) for d in range(16)]
    copies.append(pltpu.make_async_copy(img_in, img, sems.at[16]))
    for copy in copies:
        copy.start()
    for d in range(8):
        copies[2 * d].wait()
        copies[2 * d + 1].wait()
        texts[80 * d : 80 * d + 80, :] = jnp.concatenate([parts[2 * d], parts[2 * d + 1]])
    copies[16].wait()
    scale, offset = scalars[0], scalars[1]
    dots = lax.dot_general(img[...], texts[...], (((1,), (1,)), ((), ())), preferred_element_type=F32)
    rows = lax.broadcasted_iota(jnp.int32, (640, 640), 0) - place[0] * 40
    cols = lax.broadcasted_iota(jnp.int32, (640, 640), 1) - 320
    sign = jnp.where((rows == cols) & (cols >= 0) & (cols < 40), F32(1.0), F32(-1.0))
    value = (-sign * scale * jax.nn.sigmoid(-sign * (scale * dots + offset))).astype(BF)
    coef[...] = value
    coef_t[...] = value.T
    sends = [
        pltpu.make_async_copy(t_oth, to_oth, out_sems.at[0]),
        pltpu.make_async_copy(t_own, to_own, out_sems.at[1]),
        pltpu.make_async_copy(g_img.at[pl.ds(0, 320)], to_img.at[pl.ds(0, 320)], out_sems.at[2]),
        pltpu.make_async_copy(g_img.at[pl.ds(320, 320)], to_img.at[pl.ds(320, 320)], out_sems.at[3]),
    ]
    t_oth[...] = jnp.dot(coef_t[:320, :], img[...], preferred_element_type=F32).astype(BF)
    sends[0].start()
    t_own[...] = jnp.dot(coef_t[320:, :], img[...], preferred_element_type=F32).astype(BF)
    sends[1].start()
    for half in range(2):
        at = 320 * half
        g_img[at : at + 320, :] = jnp.dot(
            coef[at : at + 320, :], texts[...], preferred_element_type=F32
        ).astype(BF)
        sends[2 + half].start()
    for send in sends:
        send.wait()


def block_grads(scalars, place, img, pieces):
    small = pl.BlockSpec(memory_space=pltpu.SMEM)
    large = pl.BlockSpec(memory_space=pltpu.HBM)
    return pl.pallas_call(
        block_kernel,
        out_shape=[
            jax.ShapeDtypeStruct((320, 1152), BF),
            jax.ShapeDtypeStruct((320, 1152), BF),
            jax.ShapeDtypeStruct((640, 1152), BF),
        ],
        in_specs=[small, small] + [large] * 17,
        out_specs=[large] * 3,
        scratch_shapes=[
            pltpu.VMEM((640, 1152), BF),
            pltpu.VMEM((16, 40, 1152), BF),
            pltpu.VMEM((640, 1152), BF),
            pltpu.VMEM((640, 640), BF),
            pltpu.VMEM((640, 640), BF),
            pltpu.VMEM((320, 1152), BF),
            pltpu.VMEM((320, 1152), BF),
            pltpu.VMEM((640, 1152), BF),
            pltpu.SemaphoreType.DMA((17,)),
            pltpu.SemaphoreType.DMA((4,)),
        ],
        compiler_params=pltpu.CompilerParams(vmem_limit_bytes=60 * 2**20),
        cost_estimate=pl.CostEstimate(flops=2900000000, bytes_accessed=8000000, transcendentals=400000),
    )(scalars, place, img, *pieces)


def shards(image_features, text_features, image_proj, text_proj, log_scale, bias):
    xl, y, xh, c = (lax.axis_index(a) for a in AXES[1:])
    sent = project(image_features, image_proj, text_features, text_proj)
    stacked = jnp.concatenate(lax.optimization_barrier((image_features, text_features, *sent))[:2])
    col = jnp.arange(576, dtype=jnp.int32)
    source = (col % 144) // 18 * 144 + col // 144 * 18 + col % 18

    def pick(half, rows):
        chosen = jnp.arange(1152, dtype=jnp.int32)[:, None] == (source + 72 * half)[None, :]
        return jnp.dot(rows, chosen.astype(BF), preferred_element_type=F32).astype(BF)

    keep = pick(xl, stacked)
    give = pick(1 - xl, lax.dynamic_slice_in_dim(stacked, c * 160, 160, 0))
    own = embed([sent[0], mp_shift(sent[1], 0, 1), mp_shift(sent[2], 1, 0), mp_shift(sent[3], 1, 1)], xh, c)
    r = lax.rsqrt(jnp.sum(own * own, axis=2, keepdims=True) + 1e-06)
    z = (own * r).astype(BF)
    z, keep, give = lax.optimization_barrier((z, keep, give))
    z_img, z_txt = z[0], z[1]
    r_img, r_txt = r[0], r[1]

    img = jnp.broadcast_to(z_img[None], (16, 40, 1152))
    img, z_near = lax.optimization_barrier((img, z_txt))
    img = a2a(img, PLANE).reshape(640, 1152)
    four = shift(z_near, "z", 8, 4)
    up, down = [z_near], [z_near]
    for d in range(3):
        up.append(shift(up[-1], "z", 8, 1))
        down.append(shift(down[-1], "z", 8, -1))
    txt_own = up + [four] + down[:0:-1]
    last_up, last_down, img = lax.optimization_barrier((up[3], down[3], img))
    txt_oth = [swap_core(piece) for piece in up[:3] + [last_up, four, last_down] + down[2:0:-1]]
    give, img = lax.optimization_barrier((give, img))
    come = lax.ppermute(give, "xl", [(0, 1), (1, 0)])
    place = (xl * 4 + y) * 2 + xh
    scalars = jnp.concatenate([jnp.exp(log_scale), bias])
    t_oth, t_own, g_img = block_grads(scalars, place.astype(jnp.int32).reshape(1), img, txt_oth + txt_own)
    t_oth, come = lax.optimization_barrier((t_oth, come))
    t_got = swap_core(t_oth)
    come_oth = swap_core(come)
    come = jnp.concatenate([jnp.where(c == 0, come, come_oth), jnp.where(c == 0, come_oth, come)])
    first, second = jnp.where(xl == 0, keep, come), jnp.where(xl == 0, come, keep)
    fi = jnp.concatenate([first[:160], second[:160]])
    ft = jnp.concatenate([first[160:], second[160:]])

    t_sum = t_own.astype(F32) + t_got.astype(F32)
    to = {k: t_sum[40 * (-k % 8) : 40 * (-k % 8) + 40] for k in range(-3, 5)}
    gz_txt = ring_sum(to)
    g_img = g_img.reshape(16, 40, 1152)
    gz_img = jnp.sum(a2a(g_img, PLANE).astype(F32), axis=0)

    gz = jnp.stack([gz_img, gz_txt])
    values = z.astype(F32)
    inner = jnp.sum(values * gz, axis=2, keepdims=True)
    gp_rows = (r * (gz - values * inner)).astype(BF)
    pieces = []
    for k in range(4):
        cols = [gp_rows[:, :, 256 * k + 128 * j : 256 * k + 128 * j + 128].reshape(80, 128) for j in range(2)]
        rest = [gp_rows[i, :, 1024 + 32 * k : 1056 + 32 * k] for i in (0, 1, 0, 1)]
        pieces.append(jnp.concatenate(cols + [jnp.concatenate(rest, axis=1)]))
    piece = jnp.stack(pieces)
    got = a2a(jnp.broadcast_to(piece[None], (2, 4, 200, 128)).reshape(8, 200, 128), ("xl", "xh", "c"))
    a_img, a_txt, b_img, b_txt, rest = (got[:, 40 * i : 40 * i + 40].reshape(320, 128) for i in range(5))

    def rows_dot(x, g):
        return jnp.einsum("rd,re->de", x, g, preferred_element_type=F32)

    lane, rest = lax.optimization_barrier((lax.broadcasted_iota(jnp.int32, (576, 128), 1), rest))
    w = jnp.concatenate(
        [
            rows_dot(fi, jnp.concatenate([a_img, b_img], axis=1)),
            rows_dot(ft, jnp.concatenate([a_txt, b_txt], axis=1)),
            jnp.where(lane < 32, rows_dot(fi, rest), rows_dot(ft, rest)),
        ],
        axis=1,
    ).reshape(4, 144, 640)
    def block(k):
        return lax.dynamic_index_in_dim(w, (y + k) % 4, 0, keepdims=False)

    up, down = shift(block(2).astype(BF), "y", 4, 1), shift(block(3).astype(BF), "y", 4, -1)
    up = shift((up.astype(F32) + block(1)).astype(BF), "y", 4, 1)
    w = block(0) + down.astype(F32) + up.astype(F32)
    w = jnp.sum(a2a(w.astype(BF).reshape(8, 18, 640), ("z",)).astype(F32), axis=0)
    w_img = jnp.concatenate([w[:, :256], w[:, 512:544]], axis=1)
    w_txt = jnp.concatenate([w[:, 256:512], w[:, 544:576]], axis=1)

    mine = lax.dynamic_slice_in_dim(got, xl * 4, 4, 0)
    mine = [mine[:, 40 * i : 40 * i + 40].reshape(160, 128) for i in range(5)]
    gp_img = jnp.concatenate([mine[0], mine[2], mine[4][:, :32]], axis=1)
    gp_txt = jnp.concatenate([mine[1], mine[3], mine[4][:, 32:64]], axis=1)

    def feature_part(to):
        out = [
            jnp.einsum("re,de->rd", g, lax.dynamic_slice_in_dim(p, to * 288, 288, 0), preferred_element_type=F32)
            for g, p in ((gp_img, image_proj), (gp_txt, text_proj))
        ]
        return jnp.stack(out)

    f = feature_part(xh * 2 + c)
    for dx, dc in ((0, 1), (1, 0), (1, 1)):
        other = feature_part((xh ^ dx) * 2 + (c ^ dc)).astype(BF)
        f = f + mp_shift(other, dx, dc).astype(F32)
    return f[0], f[1], w_img, w_txt


def solution(mesh):
    fine = Mesh(mesh.devices.reshape(SIZES), AXES)
    in_specs = (P(DP, None), P(DP, None), P(None, MP), P(None, MP), P(), P())
    out_specs = (P(DP, MP), P(DP, MP), P(DP, MP), P(DP, MP))
    return jax.shard_map(shards, mesh=fine, in_specs=in_specs, out_specs=out_specs, check_vma=False)
```

```python
import jax
import jax.numpy as jnp
from jax import lax
from jax.experimental import pallas as pl
from jax.experimental.pallas import tpu as pltpu
from jax.sharding import Mesh, PartitionSpec as P

AXES = ("z", "xl", "y", "xh", "c")
SIZES = (8, 2, 4, 2, 2)
DP = ("z", "xl", "y")
MP = ("xh", "c")
PLANE = ("xl", "y", "xh")
BF = jnp.bfloat16
F32 = jnp.float32


def a2a(x, axes):
    return lax.all_to_all(x, axes, 0, 0, tiled=True)


def swap_core(x):
    return lax.ppermute(x, "c", [(0, 1), (1, 0)])


def shift(x, axis, size, step):
    return lax.ppermute(x, axis, [(i, (i + step) % size) for i in range(size)])


def ring_sum(to):
    rows = to[0].shape[0]
    far_up = shift(jnp.concatenate([to[4], to[3]]).astype(BF), "z", 8, 2).astype(F32)
    far_down = shift(jnp.concatenate([to[-3], to[-2]]).astype(BF), "z", 8, -2).astype(F32)
    near = [
        shift((to[2] + far_up[:rows]).astype(BF), "z", 8, 2),
        shift((to[1] + far_up[rows:]).astype(BF), "z", 8, 1),
        shift((to[-1] + far_down[:rows]).astype(BF), "z", 8, -1),
    ]
    return to[0] + far_down[rows:] + near[0].astype(F32) + near[1].astype(F32) + near[2].astype(F32)


def mp_shift(x, dx, dc):
    pairs = [(a * 2 + b, (a ^ dx) * 2 + (b ^ dc)) for a in range(2) for b in range(2)]
    return lax.ppermute(x, MP, pairs)


def project_kernel(*refs):
    xh, c = lax.axis_index("xh"), lax.axis_index("c")
    ins, outs, held, flat, sems = refs[:4], refs[4:8], refs[8:12], refs[12], refs[13]
    copies = [pltpu.make_async_copy(ins[i], held[i], sems.at[i]) for i in range(4)]
    for copy in copies:
        copy.start()
    for i in range(2):
        copies[2 * i].wait()
        copies[2 * i + 1].wait()
        p = lax.dot_general(
            held[2 * i][...], held[2 * i + 1][...], (((1,), (1,)), ((), ())), preferred_element_type=F32
        )
        flat[i, :, :256] = p[:, :256]
        flat[i, :, 256:384] = jnp.concatenate([p[:, 256:], jnp.zeros((160, 96), F32)], axis=1)
    for d in range(4):
        at = pl.multiple_of(((xh ^ (d // 2)) * 2 + (c ^ (d % 2))) * 40, 8)
        for i in range(2):
            outs[d][80 * i : 80 * i + 40, :] = flat[i, pl.ds(at, 40), :128]
            outs[d][80 * i + 40 : 80 * i + 80, :] = flat[i, pl.ds(at, 40), 128:256]
        outs[d][160:200, :] = flat[0, pl.ds(at, 40), 256:384] + pltpu.roll(flat[1, pl.ds(at, 40), 256:384], 32, 1)


def project(image_features, image_proj, text_features, text_proj):
    return pl.pallas_call(
        project_kernel,
        out_shape=[jax.ShapeDtypeStruct((200, 128), F32)] * 4,
        in_specs=[pl.BlockSpec(memory_space=pltpu.HBM)] * 4,
        scratch_shapes=[pltpu.VMEM((160, 1152), BF), pltpu.VMEM((288, 1152), BF)] * 2
        + [pltpu.VMEM((2, 160, 384), F32), pltpu.SemaphoreType.DMA((4,))],
        compiler_params=pltpu.CompilerParams(vmem_limit_bytes=60 * 2**20),
        cost_estimate=pl.CostEstimate(flops=220000000, bytes_accessed=2500000, transcendentals=0),
    )(image_features, image_proj.T, text_features, text_proj.T)


def embed(pieces, xh, c):
    parts = []
    for a in range(2):
        for b in range(2):
            near = jnp.where(c == b, pieces[0], pieces[1])
            far = jnp.where(c == b, pieces[2], pieces[3])
            parts.append(jnp.where(xh == a, near, far))
    rows = []
    for i in range(2):
        cols = [part[80 * i + 40 * j : 80 * i + 40 * j + 40] for part in parts for j in range(2)]
        cols += [part[160:, 32 * i : 32 * i + 32] for part in parts]
        rows.append(jnp.concatenate(cols, axis=1))
    return jnp.stack(rows)


def block_kernel(scalars, place, img_in, *refs):
    pieces = refs[:16]
    to_oth, to_own, to_img, img, parts, texts, coef, coef_t, t_oth, t_own, g_img, sems, out_sems = refs[16:]
    copies = [pltpu.make_async_copy(pieces[d], parts.at[d], sems.at[d]) for d in range(16)]
    copies.append(pltpu.make_async_copy(img_in, img, sems.at[16]))
    for copy in copies:
        copy.start()
    for d in range(8):
        copies[2 * d].wait()
        copies[2 * d + 1].wait()
        texts[80 * d : 80 * d + 80, :] = jnp.concatenate([parts[2 * d], parts[2 * d + 1]])
    copies[16].wait()
    scale, offset = scalars[0], scalars[1]
    dots = lax.dot_general(img[...], texts[...], (((1,), (1,)), ((), ())), preferred_element_type=F32)
    rows = lax.broadcasted_iota(jnp.int32, (640, 640), 0) - place[0] * 40
    cols = lax.broadcasted_iota(jnp.int32, (640, 640), 1) - 320
    sign = jnp.where((rows == cols) & (cols >= 0) & (cols < 40), F32(1.0), F32(-1.0))
    value = (-sign * scale * jax.nn.sigmoid(-sign * (scale * dots + offset))).astype(BF)
    coef[...] = value
    coef_t[...] = value.T
    sends = [
        pltpu.make_async_copy(t_oth, to_oth, out_sems.at[0]),
        pltpu.make_async_copy(t_own, to_own, out_sems.at[1]),
        pltpu.make_async_copy(g_img.at[pl.ds(0, 320)], to_img.at[pl.ds(0, 320)], out_sems.at[2]),
        pltpu.make_async_copy(g_img.at[pl.ds(320, 320)], to_img.at[pl.ds(320, 320)], out_sems.at[3]),
    ]
    t_oth[...] = jnp.dot(coef_t[:320, :], img[...], preferred_element_type=F32).astype(BF)
    sends[0].start()
    t_own[...] = jnp.dot(coef_t[320:, :], img[...], preferred_element_type=F32).astype(BF)
    sends[1].start()
    for half in range(2):
        at = 320 * half
        g_img[at : at + 320, :] = jnp.dot(
            coef[at : at + 320, :], texts[...], preferred_element_type=F32
        ).astype(BF)
        sends[2 + half].start()
    for send in sends:
        send.wait()


def block_grads(scalars, place, img, pieces):
    small = pl.BlockSpec(memory_space=pltpu.SMEM)
    large = pl.BlockSpec(memory_space=pltpu.HBM)
    return pl.pallas_call(
        block_kernel,
        out_shape=[
            jax.ShapeDtypeStruct((320, 1152), BF),
            jax.ShapeDtypeStruct((320, 1152), BF),
            jax.ShapeDtypeStruct((640, 1152), BF),
        ],
        in_specs=[small, small] + [large] * 17,
        out_specs=[large] * 3,
        scratch_shapes=[
            pltpu.VMEM((640, 1152), BF),
            pltpu.VMEM((16, 40, 1152), BF),
            pltpu.VMEM((640, 1152), BF),
            pltpu.VMEM((640, 640), BF),
            pltpu.VMEM((640, 640), BF),
            pltpu.VMEM((320, 1152), BF),
            pltpu.VMEM((320, 1152), BF),
            pltpu.VMEM((640, 1152), BF),
            pltpu.SemaphoreType.DMA((17,)),
            pltpu.SemaphoreType.DMA((4,)),
        ],
        compiler_params=pltpu.CompilerParams(vmem_limit_bytes=60 * 2**20),
        cost_estimate=pl.CostEstimate(flops=2900000000, bytes_accessed=8000000, transcendentals=400000),
    )(scalars, place, img, *pieces)


def shards(image_features, text_features, image_proj, text_proj, log_scale, bias):
    xl, y, xh, c = (lax.axis_index(a) for a in AXES[1:])
    sent = project(image_features, image_proj, text_features, text_proj)
    stacked = jnp.concatenate(lax.optimization_barrier((image_features, text_features, *sent))[:2])
    col = jnp.arange(576, dtype=jnp.int32)
    source = (col % 144) // 18 * 144 + col // 144 * 18 + col % 18

    def pick(half, rows):
        chosen = jnp.arange(1152, dtype=jnp.int32)[:, None] == (source + 72 * half)[None, :]
        return jnp.dot(rows, chosen.astype(BF), preferred_element_type=F32).astype(BF)

    keep = pick(xl, stacked)
    give = pick(1 - xl, lax.dynamic_slice_in_dim(stacked, c * 160, 160, 0))
    own = embed([sent[0], mp_shift(sent[1], 0, 1), mp_shift(sent[2], 1, 0), mp_shift(sent[3], 1, 1)], xh, c)
    r = lax.rsqrt(jnp.sum(own * own, axis=2, keepdims=True) + 1e-06)
    z = (own * r).astype(BF)
    z, keep, give = lax.optimization_barrier((z, keep, give))
    z_img, z_txt = z[0], z[1]
    r_img, r_txt = r[0], r[1]

    img = jnp.broadcast_to(z_img[None], (16, 40, 1152))
    img, z_near = lax.optimization_barrier((img, z_txt))
    img = a2a(img, PLANE).reshape(640, 1152)
    four = shift(z_near, "z", 8, 4)
    up, down = [z_near], [z_near]
    for d in range(3):
        up.append(shift(up[-1], "z", 8, 1))
        down.append(shift(down[-1], "z", 8, -1))
    txt_own = up + [four] + down[:0:-1]
    last_up, last_down, img = lax.optimization_barrier((up[3], down[3], img))
    txt_oth = [swap_core(piece) for piece in up[:3] + [last_up, four, last_down] + down[2:0:-1]]
    give, img = lax.optimization_barrier((give, img))
    come = lax.ppermute(give, "xl", [(0, 1), (1, 0)])
    place = (xl * 4 + y) * 2 + xh
    scalars = jnp.concatenate([jnp.exp(log_scale), bias])
    t_oth, t_own, g_img = block_grads(scalars, place.astype(jnp.int32).reshape(1), img, txt_oth + txt_own)
    t_oth, come = lax.optimization_barrier((t_oth, come))
    t_got = swap_core(t_oth)
    come_oth = swap_core(come)
    come = jnp.concatenate([jnp.where(c == 0, come, come_oth), jnp.where(c == 0, come_oth, come)])
    first, second = jnp.where(xl == 0, keep, come), jnp.where(xl == 0, come, keep)
    fi = jnp.concatenate([first[:160], second[:160]])
    ft = jnp.concatenate([first[160:], second[160:]])

    def block_sum(k):
        at = 40 * (-k % 8)
        return t_own[at : at + 40].astype(F32) + t_got[at : at + 40].astype(F32)

    to = {k: block_sum(k) for k in range(-3, 5)}
    gz_txt = ring_sum(to)
    g_img = g_img.reshape(16, 40, 1152)
    gz_img = jnp.sum(a2a(g_img, PLANE).astype(F32), axis=0)

    gz = jnp.stack([gz_img, gz_txt])
    values = z.astype(F32)
    inner = jnp.sum(values * gz, axis=2, keepdims=True)
    gp_rows = (r * (gz - values * inner)).astype(BF)
    pieces = []
    for k in range(4):
        cols = [gp_rows[:, :, 256 * k + 128 * j : 256 * k + 128 * j + 128].reshape(80, 128) for j in range(2)]
        rest = [gp_rows[i, :, 1024 + 32 * k : 1056 + 32 * k] for i in (0, 1, 0, 1)]
        pieces.append(jnp.concatenate(cols + [jnp.concatenate(rest, axis=1)]))
    piece = jnp.stack(pieces)
    got = a2a(jnp.broadcast_to(piece[None], (2, 4, 200, 128)).reshape(8, 200, 128), ("xl", "xh", "c"))
    a_img, a_txt, b_img, b_txt, rest = (got[:, 40 * i : 40 * i + 40].reshape(320, 128) for i in range(5))

    def rows_dot(x, g):
        return jnp.einsum("rd,re->de", x, g, preferred_element_type=F32)

    lane, rest = lax.optimization_barrier((lax.broadcasted_iota(jnp.int32, (576, 128), 1), rest))
    w = jnp.concatenate(
        [
            rows_dot(fi, jnp.concatenate([a_img, b_img], axis=1)),
            rows_dot(ft, jnp.concatenate([a_txt, b_txt], axis=1)),
            jnp.where(lane < 32, rows_dot(fi, rest), rows_dot(ft, rest)),
        ],
        axis=1,
    ).reshape(4, 144, 640)
    def block(k):
        return lax.dynamic_index_in_dim(w, (y + k) % 4, 0, keepdims=False)

    up, down = shift(block(2).astype(BF), "y", 4, 1), shift(block(3).astype(BF), "y", 4, -1)
    up = shift((up.astype(F32) + block(1)).astype(BF), "y", 4, 1)
    w = block(0) + down.astype(F32) + up.astype(F32)
    w = jnp.sum(a2a(w.astype(BF).reshape(8, 18, 640), ("z",)).astype(F32), axis=0)
    w_img = jnp.concatenate([w[:, :256], w[:, 512:544]], axis=1)
    w_txt = jnp.concatenate([w[:, 256:512], w[:, 544:576]], axis=1)

    mine = lax.dynamic_slice_in_dim(got, xl * 4, 4, 0)
    mine = [mine[:, 40 * i : 40 * i + 40].reshape(160, 128) for i in range(5)]
    gp_img = jnp.concatenate([mine[0], mine[2], mine[4][:, :32]], axis=1)
    gp_txt = jnp.concatenate([mine[1], mine[3], mine[4][:, 32:64]], axis=1)

    def feature_part(to):
        out = [
            jnp.einsum("re,de->rd", g, lax.dynamic_slice_in_dim(p, to * 288, 288, 0), preferred_element_type=F32)
            for g, p in ((gp_img, image_proj), (gp_txt, text_proj))
        ]
        return jnp.stack(out)

    f = feature_part(xh * 2 + c)
    for dx, dc in ((0, 1), (1, 0), (1, 1)):
        other = feature_part((xh ^ dx) * 2 + (c ^ dc)).astype(BF)
        f = f + mp_shift(other, dx, dc).astype(F32)
    return f[0], f[1], w_img, w_txt


def solution(mesh):
    fine = Mesh(mesh.devices.reshape(SIZES), AXES)
    in_specs = (P(DP, None), P(DP, None), P(None, MP), P(None, MP), P(), P())
    out_specs = (P(DP, MP), P(DP, MP), P(DP, MP), P(DP, MP))
    return jax.shard_map(shards, mesh=fine, in_specs=in_specs, out_specs=out_specs, check_vma=False)
```

```python
import jax
import jax.numpy as jnp
from jax import lax
from jax.experimental import pallas as pl
from jax.experimental.pallas import tpu as pltpu
from jax.sharding import Mesh, PartitionSpec as P

AXES = ("z", "xl", "y", "xh", "c")
SIZES = (8, 2, 4, 2, 2)
DP = ("z", "xl", "y")
MP = ("xh", "c")
PLANE = ("xl", "y", "xh")
BF = jnp.bfloat16
F32 = jnp.float32


def a2a(x, axes):
    return lax.all_to_all(x, axes, 0, 0, tiled=True)


def swap_core(x):
    return lax.ppermute(x, "c", [(0, 1), (1, 0)])


def shift(x, axis, size, step):
    return lax.ppermute(x, axis, [(i, (i + step) % size) for i in range(size)])


def ring_sum(to):
    rows = to[0].shape[0]
    far_up = shift(jnp.concatenate([to[4], to[3]]).astype(BF), "z", 8, 2).astype(F32)
    far_down = shift(jnp.concatenate([to[-3], to[-2]]).astype(BF), "z", 8, -2).astype(F32)
    near = [
        shift((to[2] + far_up[:rows]).astype(BF), "z", 8, 2),
        shift((to[1] + far_up[rows:]).astype(BF), "z", 8, 1),
        shift((to[-1] + far_down[:rows]).astype(BF), "z", 8, -1),
    ]
    return to[0] + far_down[rows:] + near[0].astype(F32) + near[1].astype(F32) + near[2].astype(F32)


def mp_shift(x, dx, dc):
    pairs = [(a * 2 + b, (a ^ dx) * 2 + (b ^ dc)) for a in range(2) for b in range(2)]
    return lax.ppermute(x, MP, pairs)


def project_kernel(*refs):
    xh, c = lax.axis_index("xh"), lax.axis_index("c")
    ins, outs, held, flat, sems = refs[:4], refs[4:8], refs[8:12], refs[12], refs[13]
    copies = [pltpu.make_async_copy(ins[i], held[i], sems.at[i]) for i in range(4)]
    for copy in copies:
        copy.start()
    for i in range(2):
        copies[2 * i].wait()
        copies[2 * i + 1].wait()
        p = lax.dot_general(
            held[2 * i][...], held[2 * i + 1][...], (((1,), (1,)), ((), ())), preferred_element_type=F32
        )
        flat[i, :, :256] = p[:, :256]
        flat[i, :, 256:384] = jnp.concatenate([p[:, 256:], jnp.zeros((160, 96), F32)], axis=1)
    for d in range(4):
        at = pl.multiple_of(((xh ^ (d // 2)) * 2 + (c ^ (d % 2))) * 40, 8)
        for i in range(2):
            outs[d][80 * i : 80 * i + 40, :] = flat[i, pl.ds(at, 40), :128]
            outs[d][80 * i + 40 : 80 * i + 80, :] = flat[i, pl.ds(at, 40), 128:256]
        outs[d][160:200, :] = flat[0, pl.ds(at, 40), 256:384] + pltpu.roll(flat[1, pl.ds(at, 40), 256:384], 32, 1)


def project(image_features, image_proj, text_features, text_proj):
    return pl.pallas_call(
        project_kernel,
        out_shape=[jax.ShapeDtypeStruct((200, 128), F32)] * 4,
        in_specs=[pl.BlockSpec(memory_space=pltpu.HBM)] * 4,
        scratch_shapes=[pltpu.VMEM((160, 1152), BF), pltpu.VMEM((288, 1152), BF)] * 2
        + [pltpu.VMEM((2, 160, 384), F32), pltpu.SemaphoreType.DMA((4,))],
        compiler_params=pltpu.CompilerParams(vmem_limit_bytes=60 * 2**20),
        cost_estimate=pl.CostEstimate(flops=220000000, bytes_accessed=2500000, transcendentals=0),
    )(image_features, image_proj.T, text_features, text_proj.T)


def embed(pieces, xh, c):
    parts = []
    for a in range(2):
        for b in range(2):
            near = jnp.where(c == b, pieces[0], pieces[1])
            far = jnp.where(c == b, pieces[2], pieces[3])
            parts.append(jnp.where(xh == a, near, far))
    rows = []
    for i in range(2):
        cols = [part[80 * i + 40 * j : 80 * i + 40 * j + 40] for part in parts for j in range(2)]
        cols += [part[160:, 32 * i : 32 * i + 32] for part in parts]
        rows.append(jnp.concatenate(cols, axis=1))
    return jnp.stack(rows)


def block_kernel(scalars, place, img_in, *refs):
    pieces = refs[:16]
    to_oth, to_own, to_img, img, parts, texts, coef, coef_t, t_oth, t_own, g_img, sems, out_sems = refs[16:]
    copies = [pltpu.make_async_copy(pieces[d], parts.at[d], sems.at[d]) for d in range(16)]
    copies.append(pltpu.make_async_copy(img_in, img, sems.at[16]))
    for copy in copies:
        copy.start()
    for d in range(8):
        copies[2 * d].wait()
        copies[2 * d + 1].wait()
        texts[80 * d : 80 * d + 80, :] = jnp.concatenate([parts[2 * d], parts[2 * d + 1]])
    copies[16].wait()
    scale, offset = scalars[0], scalars[1]
    dots = lax.dot_general(img[...], texts[...], (((1,), (1,)), ((), ())), preferred_element_type=F32)
    rows = lax.broadcasted_iota(jnp.int32, (640, 640), 0) - place[0] * 40
    cols = lax.broadcasted_iota(jnp.int32, (640, 640), 1) - 320
    sign = jnp.where((rows == cols) & (cols >= 0) & (cols < 40), F32(1.0), F32(-1.0))
    value = (-sign * scale * jax.nn.sigmoid(-sign * (scale * dots + offset))).astype(BF)
    coef[...] = value
    coef_t[...] = value.T
    sends = [
        pltpu.make_async_copy(t_oth, to_oth, out_sems.at[0]),
        pltpu.make_async_copy(t_own, to_own, out_sems.at[1]),
        pltpu.make_async_copy(g_img.at[pl.ds(0, 320)], to_img.at[pl.ds(0, 320)], out_sems.at[2]),
        pltpu.make_async_copy(g_img.at[pl.ds(320, 320)], to_img.at[pl.ds(320, 320)], out_sems.at[3]),
    ]
    t_oth[...] = jnp.dot(coef_t[:320, :], img[...], preferred_element_type=F32).astype(BF)
    sends[0].start()
    t_own[...] = jnp.dot(coef_t[320:, :], img[...], preferred_element_type=F32).astype(BF)
    sends[1].start()
    for half in range(2):
        at = 320 * half
        g_img[at : at + 320, :] = jnp.dot(
            coef[at : at + 320, :], texts[...], preferred_element_type=F32
        ).astype(BF)
        sends[2 + half].start()
    for send in sends:
        send.wait()


def block_grads(scalars, place, img, pieces):
    small = pl.BlockSpec(memory_space=pltpu.SMEM)
    large = pl.BlockSpec(memory_space=pltpu.HBM)
    return pl.pallas_call(
        block_kernel,
        out_shape=[
            jax.ShapeDtypeStruct((320, 1152), BF),
            jax.ShapeDtypeStruct((320, 1152), BF),
            jax.ShapeDtypeStruct((640, 1152), BF),
        ],
        in_specs=[small, small] + [large] * 17,
        out_specs=[large] * 3,
        scratch_shapes=[
            pltpu.VMEM((640, 1152), BF),
            pltpu.VMEM((16, 40, 1152), BF),
            pltpu.VMEM((640, 1152), BF),
            pltpu.VMEM((640, 640), BF),
            pltpu.VMEM((640, 640), BF),
            pltpu.VMEM((320, 1152), BF),
            pltpu.VMEM((320, 1152), BF),
            pltpu.VMEM((640, 1152), BF),
            pltpu.SemaphoreType.DMA((17,)),
            pltpu.SemaphoreType.DMA((4,)),
        ],
        compiler_params=pltpu.CompilerParams(vmem_limit_bytes=60 * 2**20),
        cost_estimate=pl.CostEstimate(flops=2900000000, bytes_accessed=8000000, transcendentals=400000),
    )(scalars, place, img, *pieces)


def shards(image_features, text_features, image_proj, text_proj, log_scale, bias):
    xl, y, xh, c = (lax.axis_index(a) for a in AXES[1:])
    sent = project(image_features, image_proj, text_features, text_proj)
    stacked = jnp.concatenate(lax.optimization_barrier((image_features, text_features, *sent))[:2])
    col = jnp.arange(576, dtype=jnp.int32)
    source = (col % 144) // 18 * 144 + col // 144 * 18 + col % 18

    def pick(half, rows):
        chosen = jnp.arange(1152, dtype=jnp.int32)[:, None] == (source + 72 * half)[None, :]
        return jnp.dot(rows, chosen.astype(BF), preferred_element_type=F32).astype(BF)

    keep = pick(xl, stacked)
    give = pick(1 - xl, lax.dynamic_slice_in_dim(stacked, c * 160, 160, 0))
    own = embed([sent[0], mp_shift(sent[1], 0, 1), mp_shift(sent[2], 1, 0), mp_shift(sent[3], 1, 1)], xh, c)
    r = lax.rsqrt(jnp.sum(own * own, axis=2, keepdims=True) + 1e-06)
    z = (own * r).astype(BF)
    z, keep, give = lax.optimization_barrier((z, keep, give))
    z_img, z_txt = z[0], z[1]
    r_img, r_txt = r[0], r[1]

    img = jnp.broadcast_to(z_img[None], (16, 40, 1152))
    img, z_near = lax.optimization_barrier((img, z_txt))
    img = a2a(img, PLANE).reshape(640, 1152)
    up, down = [z_near], [z_near]
    for d in range(3):
        up.append(shift(up[-1], "z", 8, 1))
        down.append(shift(down[-1], "z", 8, -1))
    z_four, up[2], down[2] = lax.optimization_barrier((z_near, up[2], down[2]))
    four = shift(z_four, "z", 8, 4)
    txt_own = up + [four] + down[:0:-1]
    last_up, last_down, img = lax.optimization_barrier((up[3], down[3], img))
    txt_oth = [swap_core(piece) for piece in up[:3] + [last_up, four, last_down] + down[2:0:-1]]
    give, img = lax.optimization_barrier((give, img))
    come = lax.ppermute(give, "xl", [(0, 1), (1, 0)])
    place = (xl * 4 + y) * 2 + xh
    scalars = jnp.concatenate([jnp.exp(log_scale), bias])
    t_oth, t_own, g_img = block_grads(scalars, place.astype(jnp.int32).reshape(1), img, txt_oth + txt_own)
    t_oth, come = lax.optimization_barrier((t_oth, come))
    t_got = swap_core(t_oth)
    come_oth = swap_core(come)
    come = jnp.concatenate([jnp.where(c == 0, come, come_oth), jnp.where(c == 0, come_oth, come)])
    first, second = jnp.where(xl == 0, keep, come), jnp.where(xl == 0, come, keep)
    fi = jnp.concatenate([first[:160], second[:160]])
    ft = jnp.concatenate([first[160:], second[160:]])

    t_sum = t_own.astype(F32) + t_got.astype(F32)
    to = {k: t_sum[40 * (-k % 8) : 40 * (-k % 8) + 40] for k in range(-3, 5)}
    gz_txt = ring_sum(to)
    g_img = g_img.reshape(16, 40, 1152)
    gz_img = jnp.sum(a2a(g_img, PLANE).astype(F32), axis=0)

    gz = jnp.stack([gz_img, gz_txt])
    values = z.astype(F32)
    inner = jnp.sum(values * gz, axis=2, keepdims=True)
    gp_rows = (r * (gz - values * inner)).astype(BF)
    pieces = []
    for k in range(4):
        cols = [gp_rows[:, :, 256 * k + 128 * j : 256 * k + 128 * j + 128].reshape(80, 128) for j in range(2)]
        rest = [gp_rows[i, :, 1024 + 32 * k : 1056 + 32 * k] for i in (0, 1, 0, 1)]
        pieces.append(jnp.concatenate(cols + [jnp.concatenate(rest, axis=1)]))
    piece = jnp.stack(pieces)
    got = a2a(jnp.broadcast_to(piece[None], (2, 4, 200, 128)).reshape(8, 200, 128), ("xl", "xh", "c"))
    a_img, a_txt, b_img, b_txt, rest = (got[:, 40 * i : 40 * i + 40].reshape(320, 128) for i in range(5))

    def rows_dot(x, g):
        return jnp.einsum("rd,re->de", x, g, preferred_element_type=F32)

    lane, rest = lax.optimization_barrier((lax.broadcasted_iota(jnp.int32, (576, 128), 1), rest))
    w = jnp.concatenate(
        [
            rows_dot(fi, jnp.concatenate([a_img, b_img], axis=1)),
            rows_dot(ft, jnp.concatenate([a_txt, b_txt], axis=1)),
            jnp.where(lane < 32, rows_dot(fi, rest), rows_dot(ft, rest)),
        ],
        axis=1,
    ).reshape(4, 144, 640)
    def block(k):
        return lax.dynamic_index_in_dim(w, (y + k) % 4, 0, keepdims=False)

    up, down = shift(block(2).astype(BF), "y", 4, 1), shift(block(3).astype(BF), "y", 4, -1)
    up = shift((up.astype(F32) + block(1)).astype(BF), "y", 4, 1)
    w = block(0) + down.astype(F32) + up.astype(F32)
    w = jnp.sum(a2a(w.astype(BF).reshape(8, 18, 640), ("z",)).astype(F32), axis=0)
    w_img = jnp.concatenate([w[:, :256], w[:, 512:544]], axis=1)
    w_txt = jnp.concatenate([w[:, 256:512], w[:, 544:576]], axis=1)

    mine = lax.dynamic_slice_in_dim(got, xl * 4, 4, 0)
    mine = [mine[:, 40 * i : 40 * i + 40].reshape(160, 128) for i in range(5)]
    gp_img = jnp.concatenate([mine[0], mine[2], mine[4][:, :32]], axis=1)
    gp_txt = jnp.concatenate([mine[1], mine[3], mine[4][:, 32:64]], axis=1)

    def feature_part(to):
        out = [
            jnp.einsum("re,de->rd", g, lax.dynamic_slice_in_dim(p, to * 288, 288, 0), preferred_element_type=F32)
            for g, p in ((gp_img, image_proj), (gp_txt, text_proj))
        ]
        return jnp.stack(out)

    f = feature_part(xh * 2 + c)
    for dx, dc in ((0, 1), (1, 0), (1, 1)):
        other = feature_part((xh ^ dx) * 2 + (c ^ dc)).astype(BF)
        f = f + mp_shift(other, dx, dc).astype(F32)
    return f[0], f[1], w_img, w_txt


def solution(mesh):
    fine = Mesh(mesh.devices.reshape(SIZES), AXES)
    in_specs = (P(DP, None), P(DP, None), P(None, MP), P(None, MP), P(), P())
    out_specs = (P(DP, MP), P(DP, MP), P(DP, MP), P(DP, MP))
    return jax.shard_map(shards, mesh=fine, in_specs=in_specs, out_specs=out_specs, check_vma=False)
```

```python
import jax
import jax.numpy as jnp
from jax import lax
from jax.experimental import pallas as pl
from jax.experimental.pallas import tpu as pltpu
from jax.sharding import Mesh, PartitionSpec as P

AXES = ("z", "xl", "y", "xh", "c")
SIZES = (8, 2, 4, 2, 2)
DP = ("z", "xl", "y")
MP = ("xh", "c")
PLANE = ("xl", "y", "xh")
BF = jnp.bfloat16
F32 = jnp.float32


def a2a(x, axes):
    return lax.all_to_all(x, axes, 0, 0, tiled=True)


def swap_core(x):
    return lax.ppermute(x, "c", [(0, 1), (1, 0)])


def shift(x, axis, size, step):
    return lax.ppermute(x, axis, [(i, (i + step) % size) for i in range(size)])


def ring_sum(to):
    rows = to[0].shape[0]
    far_up = shift(jnp.concatenate([to[4], to[3]]).astype(BF), "z", 8, 2).astype(F32)
    far_down = shift(jnp.concatenate([to[-3], to[-2]]).astype(BF), "z", 8, -2).astype(F32)
    near = [
        shift((to[2] + far_up[:rows]).astype(BF), "z", 8, 2),
        shift((to[1] + far_up[rows:]).astype(BF), "z", 8, 1),
        shift((to[-1] + far_down[:rows]).astype(BF), "z", 8, -1),
    ]
    return to[0] + far_down[rows:] + near[0].astype(F32) + near[1].astype(F32) + near[2].astype(F32)


def mp_shift(x, dx, dc):
    pairs = [(a * 2 + b, (a ^ dx) * 2 + (b ^ dc)) for a in range(2) for b in range(2)]
    return lax.ppermute(x, MP, pairs)


def project_kernel(*refs):
    xh, c = lax.axis_index("xh"), lax.axis_index("c")
    ins, outs, held, flat, sems = refs[:4], refs[4:8], refs[8:12], refs[12], refs[13]
    copies = [pltpu.make_async_copy(ins[i], held[i], sems.at[i]) for i in range(4)]
    for copy in copies:
        copy.start()
    for i in range(2):
        copies[2 * i].wait()
        copies[2 * i + 1].wait()
        p = lax.dot_general(
            held[2 * i][...], held[2 * i + 1][...], (((1,), (1,)), ((), ())), preferred_element_type=F32
        )
        flat[i, :, :256] = p[:, :256]
        flat[i, :, 256:384] = jnp.concatenate([p[:, 256:], jnp.zeros((160, 96), F32)], axis=1)
    for d in range(4):
        at = pl.multiple_of(((xh ^ (d // 2)) * 2 + (c ^ (d % 2))) * 40, 8)
        for i in range(2):
            outs[d][80 * i : 80 * i + 40, :] = flat[i, pl.ds(at, 40), :128]
            outs[d][80 * i + 40 : 80 * i + 80, :] = flat[i, pl.ds(at, 40), 128:256]
        outs[d][160:200, :] = flat[0, pl.ds(at, 40), 256:384] + pltpu.roll(flat[1, pl.ds(at, 40), 256:384], 32, 1)


def project(image_features, image_proj, text_features, text_proj):
    return pl.pallas_call(
        project_kernel,
        out_shape=[jax.ShapeDtypeStruct((200, 128), F32)] * 4,
        in_specs=[pl.BlockSpec(memory_space=pltpu.HBM)] * 4,
        scratch_shapes=[pltpu.VMEM((160, 1152), BF), pltpu.VMEM((288, 1152), BF)] * 2
        + [pltpu.VMEM((2, 160, 384), F32), pltpu.SemaphoreType.DMA((4,))],
        compiler_params=pltpu.CompilerParams(vmem_limit_bytes=60 * 2**20),
        cost_estimate=pl.CostEstimate(flops=220000000, bytes_accessed=2500000, transcendentals=0),
    )(image_features, image_proj.T, text_features, text_proj.T)


def embed(pieces, xh, c):
    parts = []
    for a in range(2):
        for b in range(2):
            near = jnp.where(c == b, pieces[0], pieces[1])
            far = jnp.where(c == b, pieces[2], pieces[3])
            parts.append(jnp.where(xh == a, near, far))
    rows = []
    for i in range(2):
        cols = [part[80 * i + 40 * j : 80 * i + 40 * j + 40] for part in parts for j in range(2)]
        cols += [part[160:, 32 * i : 32 * i + 32] for part in parts]
        rows.append(jnp.concatenate(cols, axis=1))
    return jnp.stack(rows)


def block_kernel(scalars, place, img_in, *refs):
    pieces = refs[:16]
    to_oth, to_own, to_img, img, parts, texts, coef, coef_t, t_oth, t_own, g_img, sems, out_sems = refs[16:]
    copies = [pltpu.make_async_copy(pieces[d], parts.at[d], sems.at[d]) for d in range(16)]
    copies.append(pltpu.make_async_copy(img_in, img, sems.at[16]))
    for copy in copies:
        copy.start()
    for d in range(8):
        copies[2 * d].wait()
        copies[2 * d + 1].wait()
        texts[80 * d : 80 * d + 80, :] = jnp.concatenate([parts[2 * d], parts[2 * d + 1]])
    copies[16].wait()
    scale, offset = scalars[0], scalars[1]
    dots = lax.dot_general(img[...], texts[...], (((1,), (1,)), ((), ())), preferred_element_type=F32)
    rows = lax.broadcasted_iota(jnp.int32, (640, 640), 0) - place[0] * 40
    cols = lax.broadcasted_iota(jnp.int32, (640, 640), 1) - 320
    sign = jnp.where((rows == cols) & (cols >= 0) & (cols < 40), F32(1.0), F32(-1.0))
    value = (-sign * scale * jax.nn.sigmoid(-sign * (scale * dots + offset))).astype(BF)
    coef[...] = value
    coef_t[...] = value.T
    sends = [
        pltpu.make_async_copy(t_oth, to_oth, out_sems.at[0]),
        pltpu.make_async_copy(t_own, to_own, out_sems.at[1]),
        pltpu.make_async_copy(g_img.at[pl.ds(0, 320)], to_img.at[pl.ds(0, 320)], out_sems.at[2]),
        pltpu.make_async_copy(g_img.at[pl.ds(320, 320)], to_img.at[pl.ds(320, 320)], out_sems.at[3]),
    ]
    t_oth[...] = jnp.dot(coef_t[:320, :], img[...], preferred_element_type=F32).astype(BF)
    sends[0].start()
    t_own[...] = jnp.dot(coef_t[320:, :], img[...], preferred_element_type=F32).astype(BF)
    sends[1].start()
    for half in range(2):
        at = 320 * half
        g_img[at : at + 320, :] = jnp.dot(
            coef[at : at + 320, :], texts[...], preferred_element_type=F32
        ).astype(BF)
        sends[2 + half].start()
    for send in sends:
        send.wait()


def block_grads(scalars, place, img, pieces):
    small = pl.BlockSpec(memory_space=pltpu.SMEM)
    large = pl.BlockSpec(memory_space=pltpu.HBM)
    return pl.pallas_call(
        block_kernel,
        out_shape=[
            jax.ShapeDtypeStruct((320, 1152), BF),
            jax.ShapeDtypeStruct((320, 1152), BF),
            jax.ShapeDtypeStruct((640, 1152), BF),
        ],
        in_specs=[small, small] + [large] * 17,
        out_specs=[large] * 3,
        scratch_shapes=[
            pltpu.VMEM((640, 1152), BF),
            pltpu.VMEM((16, 40, 1152), BF),
            pltpu.VMEM((640, 1152), BF),
            pltpu.VMEM((640, 640), BF),
            pltpu.VMEM((640, 640), BF),
            pltpu.VMEM((320, 1152), BF),
            pltpu.VMEM((320, 1152), BF),
            pltpu.VMEM((640, 1152), BF),
            pltpu.SemaphoreType.DMA((17,)),
            pltpu.SemaphoreType.DMA((4,)),
        ],
        compiler_params=pltpu.CompilerParams(vmem_limit_bytes=60 * 2**20),
        cost_estimate=pl.CostEstimate(flops=2900000000, bytes_accessed=8000000, transcendentals=400000),
    )(scalars, place, img, *pieces)


def shards(image_features, text_features, image_proj, text_proj, log_scale, bias):
    xl, y, xh, c = (lax.axis_index(a) for a in AXES[1:])
    sent = project(image_features, image_proj, text_features, text_proj)
    stacked = jnp.concatenate(lax.optimization_barrier((image_features, text_features, *sent))[:2])
    col = jnp.arange(576, dtype=jnp.int32)
    source = (col % 144) // 18 * 144 + col // 144 * 18 + col % 18

    def pick(half, rows):
        chosen = jnp.arange(1152, dtype=jnp.int32)[:, None] == (source + 72 * half)[None, :]
        return jnp.dot(rows, chosen.astype(BF), preferred_element_type=F32).astype(BF)

    keep = pick(xl, stacked)
    give = pick(1 - xl, lax.dynamic_slice_in_dim(stacked, c * 160, 160, 0))
    scalars = jnp.concatenate([jnp.exp(log_scale), bias])
    own = embed([sent[0], mp_shift(sent[1], 0, 1), mp_shift(sent[2], 1, 0), mp_shift(sent[3], 1, 1)], xh, c)
    r = lax.rsqrt(jnp.sum(own * own, axis=2, keepdims=True) + 1e-06)
    z = (own * r).astype(BF)
    z, keep, give, scalars = lax.optimization_barrier((z, keep, give, scalars))
    z_img, z_txt = z[0], z[1]
    r_img, r_txt = r[0], r[1]

    img = jnp.broadcast_to(z_img[None], (16, 40, 1152))
    img, z_near = lax.optimization_barrier((img, z_txt))
    img = a2a(img, PLANE).reshape(640, 1152)
    four = shift(z_near, "z", 8, 4)
    up, down = [z_near], [z_near]
    for d in range(3):
        up.append(shift(up[-1], "z", 8, 1))
        down.append(shift(down[-1], "z", 8, -1))
    txt_own = up + [four] + down[:0:-1]
    last_up, last_down, img = lax.optimization_barrier((up[3], down[3], img))
    txt_oth = [swap_core(piece) for piece in up[:3] + [last_up, four, last_down] + down[2:0:-1]]
    give, img = lax.optimization_barrier((give, img))
    come = lax.ppermute(give, "xl", [(0, 1), (1, 0)])
    place = (xl * 4 + y) * 2 + xh
    t_oth, t_own, g_img = block_grads(scalars, place.astype(jnp.int32).reshape(1), img, txt_oth + txt_own)
    t_oth, come = lax.optimization_barrier((t_oth, come))
    t_got = swap_core(t_oth)
    come_oth = swap_core(come)
    come = jnp.concatenate([jnp.where(c == 0, come, come_oth), jnp.where(c == 0, come_oth, come)])
    first, second = jnp.where(xl == 0, keep, come), jnp.where(xl == 0, come, keep)
    fi = jnp.concatenate([first[:160], second[:160]])
    ft = jnp.concatenate([first[160:], second[160:]])

    t_sum = t_own.astype(F32) + t_got.astype(F32)
    to = {k: t_sum[40 * (-k % 8) : 40 * (-k % 8) + 40] for k in range(-3, 5)}
    gz_txt = ring_sum(to)
    g_img = g_img.reshape(16, 40, 1152)
    gz_img = jnp.sum(a2a(g_img, PLANE).astype(F32), axis=0)

    gz = jnp.stack([gz_img, gz_txt])
    values = z.astype(F32)
    inner = jnp.sum(values * gz, axis=2, keepdims=True)
    gp_rows = (r * (gz - values * inner)).astype(BF)
    pieces = []
    for k in range(4):
        cols = [gp_rows[:, :, 256 * k + 128 * j : 256 * k + 128 * j + 128].reshape(80, 128) for j in range(2)]
        rest = [gp_rows[i, :, 1024 + 32 * k : 1056 + 32 * k] for i in (0, 1, 0, 1)]
        pieces.append(jnp.concatenate(cols + [jnp.concatenate(rest, axis=1)]))
    piece = jnp.stack(pieces)
    got = a2a(jnp.broadcast_to(piece[None], (2, 4, 200, 128)).reshape(8, 200, 128), ("xl", "xh", "c"))
    a_img, a_txt, b_img, b_txt, rest = (got[:, 40 * i : 40 * i + 40].reshape(320, 128) for i in range(5))

    def rows_dot(x, g):
        return jnp.einsum("rd,re->de", x, g, preferred_element_type=F32)

    lane, rest = lax.optimization_barrier((lax.broadcasted_iota(jnp.int32, (576, 128), 1), rest))
    w = jnp.concatenate(
        [
            rows_dot(fi, jnp.concatenate([a_img, b_img], axis=1)),
            rows_dot(ft, jnp.concatenate([a_txt, b_txt], axis=1)),
            jnp.where(lane < 32, rows_dot(fi, rest), rows_dot(ft, rest)),
        ],
        axis=1,
    ).reshape(4, 144, 640)
    def block(k):
        return lax.dynamic_index_in_dim(w, (y + k) % 4, 0, keepdims=False)

    up, down = shift(block(2).astype(BF), "y", 4, 1), shift(block(3).astype(BF), "y", 4, -1)
    up = shift((up.astype(F32) + block(1)).astype(BF), "y", 4, 1)
    w = block(0) + down.astype(F32) + up.astype(F32)
    w = jnp.sum(a2a(w.astype(BF).reshape(8, 18, 640), ("z",)).astype(F32), axis=0)
    w_img = jnp.concatenate([w[:, :256], w[:, 512:544]], axis=1)
    w_txt = jnp.concatenate([w[:, 256:512], w[:, 544:576]], axis=1)

    mine = lax.dynamic_slice_in_dim(got, xl * 4, 4, 0)
    mine = [mine[:, 40 * i : 40 * i + 40].reshape(160, 128) for i in range(5)]
    gp_img = jnp.concatenate([mine[0], mine[2], mine[4][:, :32]], axis=1)
    gp_txt = jnp.concatenate([mine[1], mine[3], mine[4][:, 32:64]], axis=1)

    def feature_part(to):
        out = [
            jnp.einsum("re,de->rd", g, lax.dynamic_slice_in_dim(p, to * 288, 288, 0), preferred_element_type=F32)
            for g, p in ((gp_img, image_proj), (gp_txt, text_proj))
        ]
        return jnp.stack(out)

    f = feature_part(xh * 2 + c)
    for dx, dc in ((0, 1), (1, 0), (1, 1)):
        other = feature_part((xh ^ dx) * 2 + (c ^ dc)).astype(BF)
        f = f + mp_shift(other, dx, dc).astype(F32)
    return f[0], f[1], w_img, w_txt


def solution(mesh):
    fine = Mesh(mesh.devices.reshape(SIZES), AXES)
    in_specs = (P(DP, None), P(DP, None), P(None, MP), P(None, MP), P(), P())
    out_specs = (P(DP, MP), P(DP, MP), P(DP, MP), P(DP, MP))
    return jax.shard_map(shards, mesh=fine, in_specs=in_specs, out_specs=out_specs, check_vma=False)
```
